256 devices in a mesh: group: 8 (over z), dom: 32 (over y, x, core).
Axes of the slice: x: 4, y: 4, z: 8, core: 2. Of those that a mesh axis runs over, the one named last changes fastest.
Arguments:
- positions: float32 [3, 8388608], P(None, ('group', 'dom')), may hold values from -1 to 1
- masses: float32 [8388608], P(('group', 'dom')), may hold values from 0.002 to 0.02
- near_target: int32 [1048576], P(('group', 'dom')), may hold values from 0 to 511
- near_source: int32 [1048576], P(('group', 'dom')), may hold values from 0 to 515
- near_count: int32 [256], P(('group', 'dom')), may hold values from 1024 to 4096, as said below
- far_target: int32 [4194304], P(('group', 'dom')), may hold values from 0 to 511
- far_source: int32 [4194304], P(('group', 'dom')), may hold values from 0 to 2047, as said below
- far_class: int32 [32768], P(('group', 'dom')), may hold values from 0 to 315
- far_count: int32 [32768], P(('group', 'dom')), may hold values from 1 to 128, as said below
- export_slots: int32 [65536, 8], P(('group', 'dom')), may hold values from 0 to 511
- operators: float32 [316, 7056], replicated, may hold values from -0.625 to 0.625
Outputs:
- potential: float32 [8388608], P(('group', 'dom'))
The draws below stay inside these ranges and needn't reach their ends.
Inputs may be any that keep to these rules, and one draw needn't show every extreme that they name: Pairs at positions near_count and later of a device's list are padding; some device's list is full. `far_count`: live pairs stand first in their batch; some batch is full. `far_source`: the slot of device s holding export slot c is s * 8 + c.
All inputs are finite; a program needn't handle non-finite values.
Results may differ from the reference program's by a relative error of at most 0.0003.
Values sent between devices are 32-bit elements; how exact they have to be, the bound alone decides.
A program may use at most 192 MiB of HBM per device.

```python
import math
import jax
import jax.numpy as jnp
import numpy as np
from jax import lax

LEAF_DEV = 512
LEAF_SIZE = 64
ORDER = 6
COEFFS = 84
NCLASS = 316
CAP = 8
RIM = 2
BATCH = 128
NEAR_DEV = 4096
FAR_BATCHES = 128
FAR_DEV = 16384
PARTICLES = 8388608
N_GROUP = 8
N_DOM = 32
DEVICES = 256


def draw_near_count(key, part):
    key = jax.random.fold_in(key, 11)
    key_counts, key_place = jax.random.split(key)
    number = N_GROUP * N_DOM
    values = jax.random.randint(key_counts, (number,), NEAR_DEV // 4, NEAR_DEV + 1, dtype=jnp.int32)
    placed = jax.random.randint(key_place, (), 0, number, dtype=jnp.int32)
    return values.at[placed].set(NEAR_DEV)


def draw_far_count(key, part):
    key = jax.random.fold_in(key, 23)
    key_counts, key_place = jax.random.split(key)
    number = FAR_BATCHES * N_GROUP * N_DOM
    values = jax.random.randint(key_counts, (number,), 1, BATCH + 1, dtype=jnp.int32)
    placed = jax.random.randint(key_place, (), 0, number, dtype=jnp.int32)
    return values.at[placed].set(BATCH)


def draw_far_source(key, part):
    key = jax.random.fold_in(key, 37)
    keys = jax.random.split(key, 8)
    devices = N_GROUP * N_DOM
    number = FAR_DEV * devices
    owner = jnp.arange(number, dtype=jnp.int32) // FAR_DEV
    reach = jax.random.randint(keys[0], (number,), 1, 17, dtype=jnp.int32)
    magnitude = jax.random.randint(keys[1], (number,), 0, 1 << 20, dtype=jnp.int32) % reach + 1
    sign_bit = 2 * jax.random.randint(keys[2], (number,), 0, 2, dtype=jnp.int32) - 1
    nearby = jnp.mod(owner + sign_bit * magnitude, devices)
    distant = jax.random.randint(keys[3], (number,), 0, devices, dtype=jnp.int32)
    pick = jax.random.randint(keys[4], (number,), 0, 4, dtype=jnp.int32) < 3
    source_dev = jnp.where(pick, nearby, distant)
    slot = jax.random.randint(keys[5], (number,), 0, CAP, dtype=jnp.int32)
    values = (source_dev * CAP + slot).astype(jnp.int32)
    low_spot = jax.random.randint(keys[6], (), 0, number // 2, dtype=jnp.int32)
    high_spot = jax.random.randint(keys[7], (), number // 2, number, dtype=jnp.int32)
    values = values.at[low_spot].set(0)
    return values.at[high_spot].set(devices * CAP - 1)


def set_ends(result, rng, smallest, high):
    longest = result.shape.index(max(result.shape))
    spots = []
    for shift in (0, 1):
        where = [jax.random.randint(jax.random.fold_in(rng, axis), (), 0, length) for axis, length in enumerate(result.shape)]
        where[longest] = (where[longest] + shift) % result.shape[longest]
        spots.append(tuple(where))
    return result.at[spots[0]].set(smallest).at[spots[1]].set(high)


def block_scale(own_key, dims, cuts, low, high):
    def one(position, shards_of):
        draws = jax.random.uniform(jax.random.fold_in(jax.random.fold_in(own_key, 6), position), (shards_of,), jnp.float32, low / len(cuts), high / len(cuts))
        return jnp.repeat(jnp.exp(draws), dims[position] // shards_of).reshape((-1,) + (1,) * (len(dims) - position - 1))

    factor_of = one(*cuts[0])
    for cut in cuts[1:]:
        factor_of = factor_of * one(*cut)
    return factor_of


def bell_draw(stream_key, dims, deviation, most, kind=jnp.bfloat16):
    drawn = deviation * jax.random.normal(stream_key, dims, jnp.float32)
    return jnp.clip(drawn, min=-most, max=most).astype(kind)


def setup_inputs(seed: int = 0) -> dict:
    streams_of = jax.random.split(jax.random.key(seed), 12)
    return {
        "positions": jnp.clip(jax.random.uniform(streams_of[0], (3, PARTICLES), jnp.float32, -1.0, 1.0) * block_scale(streams_of[0], (3, PARTICLES), ((1, 256),), -0.4, 0.0), -1.0, 1.0),
        "masses": jnp.clip(jnp.exp(math.log(0.02) - 2.30258502 * jax.random.uniform(streams_of[1], (PARTICLES,), jnp.float32) ** block_scale(streams_of[1], (PARTICLES,), ((0, 256),), -0.2, 0.2)), 0.002, 0.02),
        "near_target": set_ends(jax.random.randint(streams_of[2], (NEAR_DEV * DEVICES,), 0, LEAF_DEV), jax.random.fold_in(streams_of[2], 1), 0, LEAF_DEV - 1).astype(jnp.int32),
        "near_source": set_ends(jax.random.randint(streams_of[3], (NEAR_DEV * DEVICES,), 0, LEAF_DEV + 2 * RIM), jax.random.fold_in(streams_of[3], 1), 0, (LEAF_DEV + 2 * RIM) - 1).astype(jnp.int32),
        "near_count": draw_near_count(jax.random.fold_in(streams_of[11], 71), 0),
        "far_target": set_ends(jax.random.randint(streams_of[5], (FAR_DEV * DEVICES,), 0, LEAF_DEV), jax.random.fold_in(streams_of[5], 1), 0, LEAF_DEV - 1).astype(jnp.int32),
        "far_source": draw_far_source(jax.random.fold_in(streams_of[11], 71), 0),
        "far_class": set_ends(jax.random.randint(streams_of[7], (FAR_BATCHES * DEVICES,), 0, NCLASS), jax.random.fold_in(streams_of[7], 1), 0, NCLASS - 1).astype(jnp.int32),
        "far_count": draw_far_count(jax.random.fold_in(streams_of[11], 71), 0),
        "export_slots": set_ends(jax.random.randint(streams_of[9], (DEVICES * DEVICES, CAP), 0, LEAF_DEV), jax.random.fold_in(streams_of[9], 1), 0, LEAF_DEV - 1).astype(jnp.int32),
        "operators": bell_draw(streams_of[10], (NCLASS, COEFFS * COEFFS), COEFFS ** -0.5, 0.625, jnp.float32),
    }


softening = 0.01

def exponent_table(degree_max):
    triples = []
    for degree in range(degree_max + 1):
        for first_pow in range(degree, -1, -1):
            for second_pow in range(degree - first_pow, -1, -1):
                triples.append((first_pow, second_pow, degree - first_pow - second_pow))
    return triples

def parity_signs(degree_max):
    return np.array([(-1.0) ** (triple[0] + triple[1] + triple[2]) for triple in exponent_table(degree_max)], dtype=np.float32)

def monomials(relative, degree_max):
    powers = []
    for axis_index in range(3):
        column = [jnp.ones_like(relative[axis_index])]
        for power_step in range(degree_max):
            column.append(column[-1] * relative[axis_index])
        powers.append(column)
    return jnp.stack([powers[0][triple[0]] * powers[1][triple[1]] * powers[2][triple[2]] for triple in exponent_table(degree_max)], axis=0)

def leaf_terms(positions, masses, leaf_size):
    leaf_count = positions.shape[1] // leaf_size
    placed = positions.reshape(3, leaf_count, leaf_size)
    centre = lax.optimization_barrier(jnp.mean(placed, axis=2, keepdims=True))
    monomial = monomials(placed - centre, ORDER)
    multipole = lax.optimization_barrier(jnp.sum(monomial * masses.reshape(1, leaf_count, leaf_size), axis=2))
    return (monomial, multipole)

def far_terms(multipole, received, far_target, far_source, far_class, far_count, operators):
    coeffs = multipole.shape[0]
    batches = far_class.shape[0]
    batch_size = far_target.shape[0] // batches
    operator = operators[far_class].reshape(batches, coeffs, coeffs)
    usable = (jnp.arange(batch_size, dtype=jnp.int32)[None, :] < far_count[:, None]).astype(jnp.float32)[:, :, None]
    source_rows = received[far_source].reshape(batches, batch_size, coeffs)
    target_rows = multipole.T[far_target].reshape(batches, batch_size, coeffs)
    parity_sign = jnp.asarray(parity_signs(ORDER), dtype=jnp.float32)
    to_target = jnp.einsum('nkj,nbj->nbk', operator, source_rows, precision=lax.Precision.HIGHEST) * usable
    to_source = parity_sign * jnp.einsum('nkj,nbj->nbk', operator, target_rows * parity_sign, precision=lax.Precision.HIGHEST) * usable
    local_part = jnp.zeros((multipole.shape[1], coeffs), jnp.float32).at[far_target].add(to_target.reshape(-1, coeffs))
    reaction = jnp.zeros((received.shape[0], coeffs), jnp.float32).at[far_source].add(to_source.reshape(-1, coeffs))
    return (local_part, reaction)

def near_field(own_leaves, ext_leaves, near_target, near_source, live_count):
    pair_count = near_target.shape[0]
    block_size = math.gcd(pair_count, 256)
    block_count = pair_count // block_size
    order_ids = jnp.arange(pair_count, dtype=jnp.int32).reshape(block_count, block_size)

    def one_block(totals, inputs):
        target_ids, source_ids, position_ids = inputs
        target_leaf = own_leaves[target_ids]
        source_leaf = ext_leaves[source_ids]
        offsets = target_leaf[:, :3, :, None] - source_leaf[:, :3, None, :]
        distance = lax.optimization_barrier(jnp.sum(offsets * offsets, axis=1))
        inverse = jnp.where(distance > 0.0, lax.rsqrt(distance + softening), 0.0)
        potential_part = -lax.optimization_barrier(jnp.sum(inverse * source_leaf[:, 3, None, :], axis=2))
        potential_part = potential_part * (position_ids < live_count).astype(jnp.float32)[:, None]
        return (totals.at[target_ids].add(potential_part), None)
    starting = jnp.zeros((own_leaves.shape[0], own_leaves.shape[2]), jnp.float32)
    inputs = (near_target.reshape(block_count, block_size), near_source.reshape(block_count, block_size), order_ids)
    return lax.scan(one_block, starting, inputs)[0]

def reference(positions, masses, near_target, near_source, near_count, far_target, far_source, far_class, far_count, export_slots, operators):
    devices = N_GROUP * N_DOM
    leaves = LEAF_DEV
    span = leaves * LEAF_SIZE
    device_ids = jnp.arange(devices, dtype=jnp.int32)

    def multipole_of(device):
        placed = lax.dynamic_slice_in_dim(positions, device * span, span, 1)
        weights = lax.dynamic_slice_in_dim(masses, device * span, span, 0)
        return leaf_terms(placed, weights, LEAF_SIZE)[1].T
    leaf_rows = lax.map(multipole_of, device_ids).reshape(devices * leaves, COEFFS)
    exports = export_slots.reshape(devices, devices, CAP)
    targets_far = far_target.reshape(devices, -1)
    sources_far = far_source.reshape(devices, -1)
    classes_far = far_class.reshape(devices, -1)
    counts_far = far_count.reshape(devices, -1)

    def accumulate(totals, device):
        recv_index = (exports[:, device, :] + (device_ids * leaves)[:, None]).reshape(-1).astype(jnp.int32)
        received = leaf_rows[recv_index]
        own_rows = lax.dynamic_slice_in_dim(leaf_rows, device * leaves, leaves, 0)
        local_part, reaction = far_terms(own_rows.T, received, targets_far[device], sources_far[device], classes_far[device], counts_far[device], operators)
        totals = totals.at[device * leaves + jnp.arange(leaves, dtype=jnp.int32)].add(local_part)
        totals = totals.at[recv_index].add(reaction)
        return (totals, None)
    expansions = lax.scan(accumulate, jnp.zeros((devices * leaves, COEFFS), jnp.float32), device_ids)[0]
    stacked = jnp.concatenate([positions, masses[None, :]], axis=0)
    padded = jnp.pad(stacked, ((0, 0), (RIM * LEAF_SIZE, RIM * LEAF_SIZE)))
    targets_near = near_target.reshape(devices, -1)
    sources_near = near_source.reshape(devices, -1)

    def evaluate(device):
        placed = lax.dynamic_slice_in_dim(positions, device * span, span, 1)
        weights = lax.dynamic_slice_in_dim(masses, device * span, span, 0)
        monomial = leaf_terms(placed, weights, LEAF_SIZE)[0]
        local_exp = lax.dynamic_slice_in_dim(expansions, device * leaves, leaves, 0)
        far_part = lax.optimization_barrier(jnp.sum(local_exp.T[:, :, None] * monomial, axis=0))
        own = lax.dynamic_slice_in_dim(stacked, device * span, span, 1)
        ext = lax.dynamic_slice_in_dim(padded, device * span, span + 2 * RIM * LEAF_SIZE, 1)
        own_leaves = own.reshape(4, leaves, LEAF_SIZE).transpose(1, 0, 2)
        ext_leaves = ext.reshape(4, leaves + 2 * RIM, LEAF_SIZE).transpose(1, 0, 2)
        near_part = near_field(own_leaves, ext_leaves, targets_near[device], sources_near[device], near_count[device])
        return (near_part + far_part).reshape(-1)
    return lax.map(evaluate, device_ids).reshape(-1)
```

```python
import functools

import jax
import jax.numpy as jnp
import numpy as np
from jax import lax
from jax.experimental import pallas as pl
from jax.experimental.pallas import tpu as pltpu
from jax.sharding import PartitionSpec as P

LEAF = 64
ORDER = 6
LANES = 128
SOFTENING = 0.01
ACCS = 4
GROUP = 8
MIB = 1 << 20


def exponent_table(degree_max):
    triples = []
    for degree in range(degree_max + 1):
        for first_pow in range(degree, -1, -1):
            for second_pow in range(degree - first_pow, -1, -1):
                triples.append((first_pow, second_pow, degree - first_pow - second_pow))
    return triples


TRIPLES = exponent_table(ORDER)
COEFFS = len(TRIPLES)
INDEX = {triple: k for k, triple in enumerate(TRIPLES)}
SIGNS = np.ones((1, LANES), np.float32)
SIGNS[0, :COEFFS] = [(-1.0) ** sum(triple) for triple in TRIPLES]


def split(value):
    high = value.astype(jnp.bfloat16)
    return high, (value - high.astype(jnp.float32)).astype(jnp.bfloat16)


def dot_t(a, b):
    return lax.dot_general(a, b, (((1,), (1,)), ((), ())), preferred_element_type=jnp.float32)


def lane_id(shape):
    return lax.broadcasted_iota(jnp.int32, shape, len(shape) - 1)


def walk(x, y, z, start, visit):
    along_x = start
    for a in range(ORDER + 1):
        along_y = along_x
        for b in range(ORDER + 1 - a):
            along_z = along_y
            for c in range(ORDER + 1 - a - b):
                visit(INDEX[(a, b, c)], along_z)
                if c < ORDER - a - b:
                    along_z = along_z * z
            if b < ORDER - a:
                along_y = along_y * y
        if a < ORDER:
            along_x = along_x * x


def multipole_kernel(slots, pos, mass, table, exports, turned, terms):
    rows = mass.shape[0]
    for c in range(3):
        turned[c] = pos[c].T
    turned[3] = mass[...].T
    terms[...] = jnp.zeros_like(terms)
    for half in range(2):
        for block in range(rows // LANES):
            here = (slice(half * LEAF, (half + 1) * LEAF), slice(block * LANES, (block + 1) * LANES))
            u = []
            for c in range(3):
                value = turned[(c,) + here]
                u.append(value - jnp.sum(value, axis=0, keepdims=True) * (1.0 / LEAF))

            def visit(k, value, half=half, here=here):
                terms[half, k : k + 1, here[1]] = jnp.sum(value, axis=0, keepdims=True)

            walk(*u, turned[(3,) + here], visit)
    for half in range(2):
        table[pl.ds(half, rows, 2), :] = terms[half].T

    def export(group, carry):
        for i in range(GROUP):
            place = group * GROUP + i
            exports[pl.ds(place, 1), :] = table[pl.ds(slots[place], 1), :]
        return carry

    lax.fori_loop(0, exports.shape[0] // GROUP, export, 0)


def operator_kernel(classes, operators, out, rows, sem):
    batches = rows.shape[0]

    def copy(n):
        return pltpu.make_async_copy(operators.at[pl.ds(classes[n], 1), :], rows.at[pl.ds(n, 1), :], sem)

    lax.fori_loop(0, batches, lambda n, c: (copy(n).start(), c)[1], 0)
    lax.fori_loop(0, batches, lambda n, c: (copy(n).wait(), c)[1], 0)
    lane = lane_id((GROUP, LANES))

    def spread(group, carry):
        here = pl.ds(pl.multiple_of(group * GROUP, GROUP), GROUP)
        for k in range(COEFFS):
            first, offset = divmod(k * COEFFS, LANES)
            width = rows.shape[1]
            value = rows[here, first * LANES : min((first + 1) * LANES, width)]
            if value.shape[1] < LANES:
                value = jnp.concatenate([value, jnp.zeros((GROUP, LANES - value.shape[1]), jnp.float32)], axis=1)
            if offset:
                value = pltpu.roll(value, LANES - offset, 1)
            if offset + COEFFS > LANES:
                later = rows[here, (first + 1) * LANES : min((first + 2) * LANES, width)]
                if later.shape[1] < LANES:
                    later = jnp.concatenate(
                        [later, jnp.zeros((GROUP, LANES - later.shape[1]), jnp.float32)], axis=1
                    )
                value = jnp.where(lane < LANES - offset, value, pltpu.roll(later, LANES - offset, 1))
            out[here, k, :] = jnp.where(lane < COEFFS, value, 0.0)
        return carry

    lax.fori_loop(0, batches // GROUP, spread, 0)
    out[:, COEFFS:, :] = jnp.zeros((batches, LANES - COEFFS, LANES), jnp.float32)


def far_kernel(signed, counts, sources, targets, signs, table, matrix, out, held, *totals):
    batches = matrix.shape[0]
    size = held.shape[0] // batches

    def gather(n, carry):
        def step(group, carry):
            first = n * size + group * GROUP
            for i in range(GROUP):
                held[pl.ds(first + i, 1), :] = table[pl.ds(sources[first + i], 1), :]
            return carry

        return lax.fori_loop(0, (counts[n] + GROUP - 1) // GROUP, step, carry)

    lax.fori_loop(0, batches, gather, 0)
    row = lax.broadcasted_iota(jnp.int32, (size, LANES), 0)

    def product(n, carry):
        here = pl.ds(pl.multiple_of(n * size, size), size)
        value = jnp.where(row < counts[n], held[here, :], 0.0)
        if signed:
            value = value * signs[...]
        high, low = split(value)
        matrix_high, matrix_low = split(matrix[n])
        result = dot_t(high, matrix_high) + dot_t(low, matrix_high) + dot_t(high, matrix_low)
        held[here, :] = result * signs[...] if signed else result
        return carry

    lax.fori_loop(0, batches, product, 0, unroll=4)
    for total in totals:
        total[...] = jnp.zeros_like(total)

    def scatter(n, carry):
        def step(group, carry):
            first = n * size + group * GROUP
            for i in range(GROUP):
                total = totals[i % len(totals)]
                there = pl.ds(targets[first + i], 1)
                total[there, :] = total[there, :] + held[pl.ds(first + i, 1), :]
            return carry

        return lax.fori_loop(0, (counts[n] + GROUP - 1) // GROUP, step, carry)

    lax.fori_loop(0, batches, scatter, 0)
    out[...] = functools.reduce(lambda a, b: a + b, [total[...] for total in totals])


def near_kernel(targets, sources, count, pos, mass, before, after, out, extended, mixed, ahead, source, target, total):
    rows = mass.shape[0]
    lane = lane_id((GROUP, LANES))
    wide = lane_id((rows, LANES))
    for c in range(4):
        own = pos[c] if c < 3 else mass[...]
        extended[c, rows : extended.shape[1], :] = jnp.zeros((extended.shape[1] - rows, LANES), jnp.float32)
        extended[c, 1 : rows + 1, :] = own
        extended[c, 0:1, :] = before[c : c + 1, :]
        extended[c, rows + 1 : rows + 2, :] = after[c : c + 1, :]
        if c < 3:
            swapped = pltpu.roll(own, LEAF, 1)
            ahead[c, pl.ds(0, rows, 2), :] = jnp.where(wide < LEAF, own, swapped)
            ahead[c, pl.ds(1, rows, 2), :] = jnp.where(wide < LEAF, swapped, own)
    for c in range(4):
        for block in range(mixed.shape[0]):
            turned = extended[c, (block // 2) * LANES : (block // 2 + 1) * LANES, :].T
            for parity in range(2):
                for q in range(4):
                    first = parity * LEAF + q * GROUP
                    low = turned[first : first + GROUP]
                    high = turned[first + LEAF // 2 : first + LEAF // 2 + GROUP]
                    if block % 2:
                        low = pltpu.roll(low, LEAF, 1)
                    else:
                        high = pltpu.roll(high, LEAF, 1)
                    mixed[block, parity, c * 4 + q] = jnp.where(lane < LEAF, low, high)
    base = jnp.where(lane < LEAF, 0, LEAF)

    def spread(r, carry):
        pick = base + r % LEAF
        for parity in range(2):
            for part in range(16):
                source[2 * r + parity, part] = jnp.take_along_axis(mixed[r // LEAF, parity, part], pick, axis=1)
        return carry

    lax.fori_loop(0, rows + 2, spread, 0)

    def spread_target(leaf, carry):
        for c in range(3):
            target[leaf, c] = jnp.broadcast_to(ahead[c, pl.ds(leaf, 1), :], (GROUP, LANES))
        return carry

    lax.fori_loop(0, 2 * rows, spread_target, 0, unroll=4)
    total[...] = jnp.zeros_like(total)

    def pair(j):
        here, there = targets[j], sources[j]
        x, y, z = target[here, 0], target[here, 1], target[here, 2]
        parts = []
        for q in range(4):
            dx = x - source[there, q]
            dy = y - source[there, 4 + q]
            dz = z - source[there, 8 + q]
            distance = dx * dx + dy * dy + dz * dz
            inverse = jnp.where(distance > 0.0, lax.rsqrt(distance + SOFTENING), 0.0)
            parts.append(inverse * source[there, 12 + q])
        return here, (parts[0] + parts[1]) + (parts[2] + parts[3])

    def several(group, carry):
        done = [pair(group * GROUP + i) for i in range(GROUP)]
        for here, value in done:
            total[here] = total[here] + value
        return carry

    def single(j, carry):
        here, value = pair(j)
        total[here] = total[here] + value
        return carry

    live = count[0]
    full = live // GROUP
    lax.fori_loop(0, full, several, 0)
    lax.fori_loop(full * GROUP, live, single, 0)
    summed = jnp.sum(total[...], axis=1)
    ahead[0] = summed + pltpu.roll(summed, LEAF, 1)
    out[...] = -jnp.where(wide < LEAF, ahead[0, pl.ds(0, rows, 2), :], ahead[0, pl.ds(1, rows, 2), :])


def evaluate_kernel(pos, local, returned, slots, near, out, expansion, turned, terms):
    rows = near.shape[0]
    leaves = local.shape[0]
    chunk = slots.shape[1]
    leaf = lax.broadcasted_iota(jnp.int32, (leaves, chunk), 0)
    sums = local[...]
    for block in range(slots.shape[0]):
        hot = (leaf == slots[block : block + 1, :]).astype(jnp.float32).astype(jnp.bfloat16)
        high, low = split(returned[block * chunk : (block + 1) * chunk, :])
        sums = sums + jnp.dot(hot, high, preferred_element_type=jnp.float32)
        sums = sums + jnp.dot(hot, low, preferred_element_type=jnp.float32)
    expansion[...] = sums
    for half in range(2):
        terms[half] = expansion[pl.ds(half, rows, 2), :].T
    for c in range(3):
        turned[c] = pos[c].T
    for half in range(2):
        for block in range(rows // LANES):
            here = (slice(half * LEAF, (half + 1) * LEAF), slice(block * LANES, (block + 1) * LANES))
            u = []
            for c in range(3):
                value = turned[(c,) + here]
                u.append(value - jnp.sum(value, axis=0, keepdims=True) * (1.0 / LEAF))
            sums = [jnp.zeros((LEAF, LANES), jnp.float32)]

            def visit(k, value, half=half, here=here, sums=sums):
                sums[0] = sums[0] + value * terms[half, k : k + 1, here[1]]

            walk(*u, jnp.ones((LEAF, LANES), jnp.float32), visit)
            turned[(3,) + here] = sums[0]
    out[...] = near[...] + turned[3].T


VMEM = pl.BlockSpec(memory_space=pltpu.VMEM)
SMEM = pl.BlockSpec(memory_space=pltpu.SMEM)
ANY = pl.BlockSpec(memory_space=pl.ANY)


def shape(*dims):
    return jax.ShapeDtypeStruct(dims, jnp.float32)


def params(mib):
    return pltpu.CompilerParams(vmem_limit_bytes=mib * MIB)


def multipoles(pos, mass, slots):
    rows = mass.shape[0]
    return pl.pallas_call(
        multipole_kernel,
        out_shape=(shape(2 * rows, LANES), shape(slots.shape[0], LANES)),
        in_specs=[SMEM, VMEM, VMEM],
        out_specs=(VMEM, VMEM),
        scratch_shapes=[pltpu.VMEM((4, LANES, rows), jnp.float32), pltpu.VMEM((2, LANES, rows), jnp.float32)],
        compiler_params=params(32),
        name="multipoles",
    )(slots, pos, mass)


def operator_matrices(classes, operators):
    batches = classes.shape[0]
    return pl.pallas_call(
        operator_kernel,
        out_shape=shape(batches, LANES, LANES),
        in_specs=[SMEM, ANY],
        out_specs=VMEM,
        scratch_shapes=[pltpu.VMEM((batches, operators.shape[1]), jnp.float32), pltpu.SemaphoreType.DMA],
        compiler_params=params(32),
        name="operator_matrices",
    )(classes, operators)


def far(signed, counts, sources, targets, table, matrix, out_rows, name):
    return pl.pallas_call(
        functools.partial(far_kernel, signed),
        out_shape=shape(out_rows, LANES),
        in_specs=[SMEM, SMEM, SMEM, VMEM, VMEM, VMEM],
        out_specs=VMEM,
        scratch_shapes=[pltpu.VMEM((sources.shape[0], LANES), jnp.float32)]
        + [pltpu.VMEM((out_rows, LANES), jnp.float32)] * ACCS,
        compiler_params=params(48),
        name=name,
    )(counts, sources, targets, jnp.asarray(SIGNS), table, matrix)


def near_field(targets, sources, count, pos, mass, before, after):
    rows = mass.shape[0]
    blocks = -(-(rows + 2) // LEAF)
    return pl.pallas_call(
        near_kernel,
        out_shape=shape(rows, LANES),
        in_specs=[SMEM, SMEM, SMEM, VMEM, VMEM, VMEM, VMEM],
        out_specs=VMEM,
        scratch_shapes=[
            pltpu.VMEM((4, (blocks + 1) // 2 * LANES, LANES), jnp.float32),
            pltpu.VMEM((blocks, 2, 16, GROUP, LANES), jnp.float32),
            pltpu.VMEM((3, 2 * rows, LANES), jnp.float32),
            pltpu.VMEM((2 * rows + 4, 16, GROUP, LANES), jnp.float32),
            pltpu.VMEM((2 * rows, 3, GROUP, LANES), jnp.float32),
            pltpu.VMEM((2 * rows, GROUP, LANES), jnp.float32),
        ],
        compiler_params=params(58),
        name="near_field",
    )(targets, sources, count, pos, mass, before, after)


def evaluate(pos, local, returned, slots, near):
    rows = near.shape[0]
    return pl.pallas_call(
        evaluate_kernel,
        out_shape=shape(rows, LANES),
        in_specs=[VMEM] * 5,
        out_specs=VMEM,
        scratch_shapes=[
            pltpu.VMEM((2 * rows, LANES), jnp.float32),
            pltpu.VMEM((4, LANES, rows), jnp.float32),
            pltpu.VMEM((2, LANES, rows), jnp.float32),
        ],
        compiler_params=params(32),
        name="evaluate",
    )(pos, local, returned, slots, near)


AXES = ("group", "dom")


def exchange(value):
    return lax.all_to_all(value, AXES, split_axis=0, concat_axis=0, tiled=True)


def shift(value, forward):
    count = lax.axis_size("group") * lax.axis_size("dom")
    pairs = [(i, i + 1) for i in range(count - 1)] if forward else [(i + 1, i) for i in range(count - 1)]
    return lax.ppermute(value, AXES, pairs)


def local(
    positions,
    masses,
    near_target,
    near_source,
    near_count,
    far_target,
    far_source,
    far_class,
    far_count,
    export_slots,
    operators,
):
    devices = lax.axis_size("group") * lax.axis_size("dom")
    slots = export_slots.reshape(-1)
    pos = positions.reshape(3, -1, LANES)
    mass = masses.reshape(-1, LANES)
    leaves = masses.shape[0] // LEAF
    ends = jnp.concatenate([pos[:, :: mass.shape[0] - 1], mass[None, :: mass.shape[0] - 1]], axis=0)
    before = shift(ends[:, 1], True)
    after = shift(ends[:, 0], False)
    table, exports = multipoles(pos, mass, slots)
    received = exchange(exports.reshape(devices, -1, LANES)).reshape(-1, LANES)
    matrix = operator_matrices(far_class, operators)
    reaction = far(True, far_count, far_target, far_source, table, matrix, slots.shape[0], "far_reaction")
    returned = exchange(reaction.reshape(devices, -1, LANES)).reshape(-1, LANES)
    near = near_field(near_target, near_source, near_count, pos, mass, before, after)
    local_part = far(False, far_count, far_source, far_target, received, matrix, leaves, "far_local")
    out = evaluate(pos, local_part, returned, slots.reshape(8, -1), near)
    return out.reshape(-1)


def solution(mesh):
    split_all = P(AXES)
    in_specs = (P(None, AXES),) + (split_all,) * 8 + (P(AXES, None), P())
    return jax.shard_map(local, mesh=mesh, in_specs=in_specs, out_specs=split_all, check_vma=False)
```

```python
import functools

import jax
import jax.numpy as jnp
import numpy as np
from jax import lax
from jax.experimental import pallas as pl
from jax.experimental.pallas import tpu as pltpu
from jax.sharding import PartitionSpec as P

LEAF = 64
ORDER = 6
LANES = 128
SOFTENING = 0.01
ACCS = 8
GROUP = 8
ROWS = 16
PAIRS = 16
JOINT = 4
MIB = 1 << 20


def exponent_table(degree_max):
    triples = []
    for degree in range(degree_max + 1):
        for first_pow in range(degree, -1, -1):
            for second_pow in range(degree - first_pow, -1, -1):
                triples.append((first_pow, second_pow, degree - first_pow - second_pow))
    return triples


TRIPLES = exponent_table(ORDER)
COEFFS = len(TRIPLES)
INDEX = {triple: k for k, triple in enumerate(TRIPLES)}
SIGNS = np.ones((1, LANES), np.float32)
SIGNS[0, :COEFFS] = [(-1.0) ** sum(triple) for triple in TRIPLES]


def split(value):
    high = value.astype(jnp.bfloat16)
    return high, (value - high.astype(jnp.float32)).astype(jnp.bfloat16)


def dot_t(a, b):
    return lax.dot_general(a, b, (((1,), (1,)), ((), ())), preferred_element_type=jnp.float32)


def lane_id(shape):
    return lax.broadcasted_iota(jnp.int32, shape, len(shape) - 1)


def walk(x, y, z, start, visit):
    along_x = start
    for a in range(ORDER + 1):
        along_y = along_x
        for b in range(ORDER + 1 - a):
            along_z = along_y
            for c in range(ORDER + 1 - a - b):
                visit(INDEX[(a, b, c)], along_z)
                if c < ORDER - a - b:
                    along_z = along_z * z
            if b < ORDER - a:
                along_y = along_y * y
        if a < ORDER:
            along_x = along_x * x


def centred(turned, here):
    u = []
    for c in range(3):
        value = turned[(c,) + here]
        u.append(value - jnp.sum(value, axis=0, keepdims=True) * (1.0 / LEAF))
    return u


def blocks_of(rows):
    for half in range(2):
        for block in range(rows // LANES):
            yield half, (slice(half * LEAF, (half + 1) * LEAF), slice(block * LANES, (block + 1) * LANES))


def list_groups(counts, batches, size, groups):
    def one(n, place):
        for i in range(size // ROWS):
            groups[place + i] = n * size + i * ROWS
        return place + (counts[n] + ROWS - 1) // ROWS

    return lax.fori_loop(0, batches, one, 0)


def each_group(groups, number, step):
    def several(turn, carry):
        step([groups[turn * JOINT + i] for i in range(JOINT)])
        return carry

    def single(turn, carry):
        step([groups[turn]])
        return carry

    lax.fori_loop(0, number // JOINT, several, 0)
    lax.fori_loop(number // JOINT * JOINT, number, single, 0)


def views(index):
    return [index.at[pl.ds(i, index.shape[0] - ROWS + 1)] for i in range(ROWS)]


def gather_rows(groups, number, index, table, held):
    later = views(index)

    def step(firsts):
        for first in firsts:
            rows = [table[pl.ds(later[i][first], 1), :] for i in range(ROWS)]
            for i in range(ROWS):
                held[pl.ds(first + i, 1), :] = rows[i]

    each_group(groups, number, step)


def scatter_rows(groups, number, index, held, totals):
    for total in totals:
        total[...] = jnp.zeros_like(total)

    later = views(index)

    def step(firsts):
        for first in firsts:
            for i in range(ROWS):
                total = totals[i % len(totals)]
                there = pl.ds(later[i][first], 1)
                total[there, :] = total[there, :] + held[pl.ds(first + i, 1), :]

    each_group(groups, number, step)


def sum_of(totals):
    return functools.reduce(lambda a, b: a + b, [total[...] for total in totals])


def multiply(value, both):
    high, low = split(value)
    wide = dot_t(high, both)
    return wide[:, :LANES] + wide[:, LANES:] + dot_t(low, both[:LANES])


def front_kernel(
    slots, classes, counts, targets, sources, signs, pos, mass, operators,
    message, packed,
    turned, terms, table, rows, matrix, both, held, *rest,
):
    *totals, groups, row_sem, out_sem = rest
    batches = rows.shape[0]
    size = held.shape[0] // batches
    leaf_rows = mass.shape[0]

    def fetch(n):
        return pltpu.make_async_copy(operators.at[pl.ds(classes[n], 1), :], rows.at[pl.ds(n, 1), :], row_sem)

    lax.fori_loop(0, batches, lambda n, c: (fetch(n).start(), c)[1], 0)
    for c in range(3):
        turned[c] = pos[c].T
    turned[3] = mass[...].T
    terms[...] = jnp.zeros_like(terms)
    for half, here in blocks_of(leaf_rows):

        def visit(k, value, half=half, here=here):
            terms[half, k : k + 1, here[1]] = jnp.sum(value, axis=0, keepdims=True)

        walk(*centred(turned, here), turned[(3,) + here], visit)
    for half in range(2):
        table[pl.ds(half, leaf_rows, 2), :] = terms[half].T
    cap = message.shape[1] // 2

    later = views(slots)

    def export(group, carry):
        values = [table[pl.ds(later[i][group * ROWS], 1), :] for i in range(ROWS)]
        for i in range(ROWS):
            message[group * (ROWS // cap) + i // cap, i % cap : i % cap + 1, :] = values[i]
        return carry

    lax.fori_loop(0, slots.shape[0] // ROWS, export, 0)
    number = list_groups(counts, batches, size, groups)
    gather_rows(groups, number, targets, table, held)
    lax.fori_loop(0, batches, lambda n, c: (fetch(n).wait(), c)[1], 0)
    lane = lane_id((GROUP, LANES))
    width = rows.shape[1]
    matrix[:, COEFFS:, :] = jnp.zeros((batches, LANES - COEFFS, LANES), jnp.float32)

    def spread(group, carry):
        here = pl.ds(pl.multiple_of(group * GROUP, GROUP), GROUP)

        def part(first):
            value = rows[here, first * LANES : min((first + 1) * LANES, width)]
            if value.shape[1] < LANES:
                value = jnp.concatenate([value, jnp.zeros((GROUP, LANES - value.shape[1]), jnp.float32)], axis=1)
            return value

        for k in range(COEFFS):
            first, offset = divmod(k * COEFFS, LANES)
            value = part(first)
            if offset + COEFFS > LANES:
                value = jnp.where(lane < offset, part(first + 1), value)
            if offset:
                value = pltpu.roll(value, LANES - offset, 1)
            matrix[here, k, :] = jnp.where(lane < COEFFS, value, 0.0)
        return carry

    lax.fori_loop(0, batches // GROUP, spread, 0)
    row = lax.broadcasted_iota(jnp.int32, (size, LANES), 0)

    def product(n, carry):
        here = pl.ds(pl.multiple_of(n * size, size), size)
        value = jnp.where(row < counts[n], held[here, :], 0.0) * signs[...]
        high, low = split(matrix[n])
        both[n, :LANES] = high
        both[n, LANES:] = low
        held[here, :] = multiply(value, jnp.concatenate([high, low], axis=0))
        return carry

    lax.fori_loop(0, batches, product, 0, unroll=8)
    save = pltpu.make_async_copy(both, packed, out_sem)
    save.start()
    scatter_rows(groups, number, sources, held, totals)
    message[:, cap:, :] = (sum_of(totals) * signs[...]).reshape(message.shape[0], cap, LANES)
    save.wait()


def near_kernel(targets, sources, count, pos, mass, before, after, out, extended, lines, choose, ahead, source, target, total):
    rows = mass.shape[0]
    wide = lane_id((rows, LANES))
    for c in range(4):
        own = pos[c] if c < 3 else mass[...]
        extended[c, rows : extended.shape[1], :] = jnp.zeros((extended.shape[1] - rows, LANES), jnp.float32)
        extended[c, 1 : rows + 1, :] = own
        extended[c, 0:1, :] = before[c : c + 1, :]
        extended[c, rows + 1 : rows + 2, :] = after[c : c + 1, :]
        if c < 3:
            swapped = pltpu.roll(own, LEAF, 1)
            ahead[c, pl.ds(0, rows, 2), :] = jnp.where(wide < LEAF, own, swapped)
            ahead[c, pl.ds(1, rows, 2), :] = jnp.where(wide < LEAF, swapped, own)
    k_id = lax.broadcasted_iota(jnp.int32, (2 * LANES, 2 * LANES), 0)
    n_id = lax.broadcasted_iota(jnp.int32, (2 * LANES, 2 * LANES), 1)
    k_in = k_id % LANES
    code = (k_in // (3 * GROUP)) * GROUP + k_in % GROUP - n_id // LANES * GROUP
    code = jnp.where(k_id // LANES == n_id % LANES // LEAF, code, -1)
    tiles = choose.shape[0]

    def make_choice(tile, carry):
        wanted = tile // GROUP * 2 * GROUP + tile % GROUP
        choose[tile] = (code == wanted).astype(jnp.float32).astype(jnp.bfloat16)
        return carry

    lax.fori_loop(0, tiles, make_choice, 0)
    blocks = lines.shape[0] // LEAF
    for block in range(blocks):
        parts = []
        for c in range(4):
            value = extended[c, block * GROUP : (block + 1) * GROUP, :]
            for _ in range(2):
                high = value.astype(jnp.bfloat16).astype(jnp.float32)
                parts.append(high)
                value = value - high
            parts.append(value)
        parts.append(jnp.zeros((LANES - 12 * GROUP, LANES), jnp.float32))
        turned = jnp.concatenate(parts, axis=0).T.astype(jnp.bfloat16)
        quarter = LEAF // 2
        for parity in range(2):
            there = slice(block * LEAF + parity * quarter, block * LEAF + (parity + 1) * quarter)
            lines[there, :LANES] = turned[parity * LEAF : parity * LEAF + quarter]
            lines[there, LANES:] = turned[parity * LEAF + quarter : (parity + 1) * LEAF]
    share = blocks // 3

    def spread(step, carry):
        tile, third = step % tiles, step // tiles
        pair_of, r = tile // GROUP, tile % GROUP
        size = share * LEAF
        some = lines[pl.ds(pl.multiple_of(third * size, size), size), :]
        wide = jnp.dot(some, choose[tile], preferred_element_type=jnp.float32)
        for i in range(share):
            for parity in range(2):
                for q in range(4):
                    first = i * LEAF + parity * 32 + q * GROUP
                    leaf = 2 * ((third * share + i) * GROUP + r) + parity
                    for c in range(2):
                        source[leaf, (2 * pair_of + c) * 4 + q] = wide[first : first + GROUP, c * LANES : (c + 1) * LANES]
        return carry

    lax.fori_loop(0, 3 * tiles, spread, 0, unroll=2)

    def spread_target(leaf, carry):
        for c in range(3):
            target[leaf, c] = jnp.broadcast_to(ahead[c, pl.ds(leaf, 1), :], (GROUP, LANES))
        return carry

    lax.fori_loop(0, 2 * rows, spread_target, 0, unroll=4)
    total[...] = jnp.zeros_like(total)

    def pair(here, there):
        x, y, z = target[here, 0], target[here, 1], target[here, 2]
        parts = []
        for q in range(4):
            dx = x - source[there, q]
            dy = y - source[there, 4 + q]
            dz = z - source[there, 8 + q]
            distance = dx * dx + dy * dy + dz * dz
            inverse = jnp.where(distance > 0.0, lax.rsqrt(distance + SOFTENING), 0.0)
            parts.append(inverse * source[there, 12 + q])
        return here, (parts[0] + parts[1]) + (parts[2] + parts[3])

    later_target, later_source = views(targets), views(sources)

    def several(group, carry):
        first = group * PAIRS
        done = [pair(later_target[i][first], later_source[i][first]) for i in range(PAIRS)]
        for here, value in done:
            total[here] = total[here] + value
        return carry

    def single(j, carry):
        here, value = pair(targets[j], sources[j])
        total[here] = total[here] + value
        return carry

    live = count[0]
    full = live // PAIRS
    lax.fori_loop(0, full, several, 0)
    lax.fori_loop(full * PAIRS, live, single, 0)
    summed = jnp.sum(total[...], axis=1)
    ahead[0] = summed + pltpu.roll(summed, LEAF, 1)
    out[...] = -jnp.where(wide < LEAF, ahead[0, pl.ds(0, rows, 2), :], ahead[0, pl.ds(1, rows, 2), :])


def back_kernel(
    counts, sources, targets, slots, pos, near, packed, message,
    out,
    table, returned, both, held, expansion, turned, terms, *rest,
):
    *totals, groups, matrix_sem, table_sem, returned_sem = rest
    cap = table.shape[1]
    batches = both.shape[0]
    size = held.shape[0] // batches
    rows = near.shape[0]
    fetch_table = pltpu.make_async_copy(message.at[:, :cap, :], table, table_sem)
    fetch_table.start()
    fetch_returned = pltpu.make_async_copy(message.at[:, cap:, :], returned, returned_sem)
    fetch_returned.start()
    fetch_matrix = pltpu.make_async_copy(packed, both, matrix_sem)
    fetch_matrix.start()
    for c in range(3):
        turned[c] = pos[c].T
    number = list_groups(counts, batches, size, groups)
    fetch_table.wait()
    gather_rows(groups, number, sources, table.reshape(table.shape[0] * cap, LANES), held)
    fetch_matrix.wait()
    row = lax.broadcasted_iota(jnp.int32, (size, LANES), 0)

    def product(n, carry):
        here = pl.ds(pl.multiple_of(n * size, size), size)
        held[here, :] = multiply(jnp.where(row < counts[n], held[here, :], 0.0), both[n])
        return carry

    lax.fori_loop(0, batches, product, 0, unroll=8)
    scatter_rows(groups, number, targets, held, totals)
    fetch_returned.wait()
    chunk = slots.shape[1]
    leaf = lax.broadcasted_iota(jnp.int32, (expansion.shape[0], chunk), 0)
    sums = sum_of(totals)
    for block in range(slots.shape[0]):
        hot = (leaf == slots[block : block + 1, :]).astype(jnp.float32).astype(jnp.bfloat16)
        part = returned[block * chunk // cap : (block + 1) * chunk // cap]
        high, low = split(part.reshape(chunk, LANES))
        sums = sums + jnp.dot(hot, high, preferred_element_type=jnp.float32)
        sums = sums + jnp.dot(hot, low, preferred_element_type=jnp.float32)
    expansion[...] = sums
    for half in range(2):
        terms[half] = expansion[pl.ds(half, rows, 2), :].T
    for half, here in blocks_of(rows):
        sums = [jnp.zeros((LEAF, LANES), jnp.float32)]

        def visit(k, value, half=half, here=here, sums=sums):
            sums[0] = sums[0] + value * terms[half, k : k + 1, here[1]]

        walk(*centred(turned, here), jnp.ones((LEAF, LANES), jnp.float32), visit)
        turned[(3,) + here] = sums[0]
    out[...] = near[...] + turned[3].T


VMEM = pl.BlockSpec(memory_space=pltpu.VMEM)
SMEM = pl.BlockSpec(memory_space=pltpu.SMEM)
ANY = pl.BlockSpec(memory_space=pl.ANY)


def shape(*dims):
    return jax.ShapeDtypeStruct(dims, jnp.float32)


def params(mib):
    return pltpu.CompilerParams(vmem_limit_bytes=mib * MIB)


def scratch(*dims, dtype=jnp.float32):
    return pltpu.VMEM(dims, dtype)


def group_list(pairs, batches):
    return pltpu.SMEM((pairs // ROWS + pairs // batches // ROWS,), jnp.int32)


def front(slots, classes, counts, targets, sources, pos, mass, operators, devices):
    rows = mass.shape[0]
    batches, pairs = classes.shape[0], targets.shape[0]
    return pl.pallas_call(
        front_kernel,
        out_shape=(
            shape(devices, 2 * slots.shape[0] // devices, LANES),
            jax.ShapeDtypeStruct((batches, 2 * LANES, LANES), jnp.bfloat16),
        ),
        in_specs=[SMEM] * 5 + [VMEM] * 3 + [ANY],
        out_specs=(VMEM, ANY),
        scratch_shapes=[
            scratch(4, LANES, rows),
            scratch(2, LANES, rows),
            scratch(2 * rows, LANES),
            scratch(batches, operators.shape[1]),
            scratch(batches, LANES, LANES),
            scratch(batches, 2 * LANES, LANES, dtype=jnp.bfloat16),
            scratch(pairs, LANES),
        ]
        + [scratch(slots.shape[0], LANES)] * ACCS
        + [group_list(pairs, batches)]
        + [pltpu.SemaphoreType.DMA] * 2,
        compiler_params=params(58),
        name="front",
    )(slots, classes, counts, targets, sources, jnp.asarray(SIGNS), pos, mass, operators)


def back(counts, sources, targets, slots, pos, near, packed, message):
    rows = near.shape[0]
    cap = message.shape[1] // 2
    return pl.pallas_call(
        back_kernel,
        out_shape=shape(rows, LANES),
        in_specs=[SMEM] * 3 + [VMEM] * 3 + [ANY] * 2,
        out_specs=VMEM,
        scratch_shapes=[
            scratch(message.shape[0], cap, LANES),
            scratch(message.shape[0], cap, LANES),
            scratch(*packed.shape, dtype=jnp.bfloat16),
            scratch(sources.shape[0], LANES),
            scratch(2 * rows, LANES),
            scratch(4, LANES, rows),
            scratch(2, LANES, rows),
        ]
        + [scratch(2 * rows, LANES)] * ACCS
        + [group_list(sources.shape[0], counts.shape[0])]
        + [pltpu.SemaphoreType.DMA] * 3,
        compiler_params=params(58),
        name="back",
    )(counts, sources, targets, slots, pos, near, packed, message)


def near_field(targets, sources, count, pos, mass, before, after):
    rows = mass.shape[0]
    blocks = -(-(rows + 2) // (3 * GROUP)) * 3
    return pl.pallas_call(
        near_kernel,
        out_shape=shape(rows, LANES),
        in_specs=[SMEM] * 3 + [VMEM] * 4,
        out_specs=VMEM,
        scratch_shapes=[
            scratch(4, blocks * GROUP, LANES),
            scratch(blocks * LEAF, 2 * LANES, dtype=jnp.bfloat16),
            scratch(2 * GROUP, 2 * LANES, 2 * LANES, dtype=jnp.bfloat16),
            scratch(3, 2 * rows, LANES),
            scratch(2 * blocks * GROUP, 16, GROUP, LANES),
            scratch(2 * rows, 3, GROUP, LANES),
            scratch(2 * rows, GROUP, LANES),
        ],
        compiler_params=params(58),
        name="near_field",
    )(targets, sources, count, pos, mass, before, after)


AXES = ("group", "dom")


def exchange(value):
    return lax.all_to_all(value, AXES, split_axis=0, concat_axis=0, tiled=True)


def shift(value, forward):
    count = lax.axis_size("group") * lax.axis_size("dom")
    pairs = [(i, i + 1) for i in range(count - 1)] if forward else [(i + 1, i) for i in range(count - 1)]
    return lax.ppermute(value, AXES, pairs)


def local(
    positions,
    masses,
    near_target,
    near_source,
    near_count,
    far_target,
    far_source,
    far_class,
    far_count,
    export_slots,
    operators,
):
    devices = lax.axis_size("group") * lax.axis_size("dom")
    slots = export_slots.reshape(-1)
    pos = positions.reshape(3, -1, LANES)
    mass = masses.reshape(-1, LANES)
    ends = jnp.concatenate([pos[:, :: mass.shape[0] - 1], mass[None, :: mass.shape[0] - 1]], axis=0)
    before = shift(ends[:, 1], True)
    after = shift(ends[:, 0], False)
    message, packed = front(slots, far_class, far_count, far_target, far_source, pos, mass, operators, devices)
    message = exchange(message)
    near = near_field(near_target, near_source, near_count, pos, mass, before, after)
    out = back(far_count, far_source, far_target, slots.reshape(8, -1), pos, near, packed, message)
    return out.reshape(-1)


def solution(mesh):
    split_all = P(AXES)
    in_specs = (P(None, AXES),) + (split_all,) * 8 + (P(AXES, None), P())
    return jax.shard_map(local, mesh=mesh, in_specs=in_specs, out_specs=split_all, check_vma=False)
```

```python
import functools

import jax
import jax.numpy as jnp
import numpy as np
from jax import lax
from jax.experimental import pallas as pl
from jax.experimental.pallas import tpu as pltpu
from jax.sharding import PartitionSpec as P

LEAF = 64
ORDER = 6
LANES = 128
SOFTENING = 0.01
ACCS = 8
GROUP = 8
ROWS = 16
PAIRS = 32
JOINT = 4
MIB = 1 << 20


def exponent_table(degree_max):
    triples = []
    for degree in range(degree_max + 1):
        for first_pow in range(degree, -1, -1):
            for second_pow in range(degree - first_pow, -1, -1):
                triples.append((first_pow, second_pow, degree - first_pow - second_pow))
    return triples


TRIPLES = exponent_table(ORDER)
COEFFS = len(TRIPLES)
INDEX = {triple: k for k, triple in enumerate(TRIPLES)}
SIGNS = np.ones((1, LANES), np.float32)
SIGNS[0, :COEFFS] = [(-1.0) ** sum(triple) for triple in TRIPLES]


def split(value):
    high = value.astype(jnp.bfloat16)
    return high, (value - high.astype(jnp.float32)).astype(jnp.bfloat16)


def lane_id(shape):
    return lax.broadcasted_iota(jnp.int32, shape, len(shape) - 1)


def walk(x, y, z, start, visit):
    along_x = start
    for a in range(ORDER + 1):
        along_y = along_x
        for b in range(ORDER + 1 - a):
            along_z = along_y
            for c in range(ORDER + 1 - a - b):
                visit(INDEX[(a, b, c)], along_z)
                if c < ORDER - a - b:
                    along_z = along_z * z
            if b < ORDER - a:
                along_y = along_y * y
        if a < ORDER:
            along_x = along_x * x


def centred(turned, here):
    u = []
    for c in range(3):
        value = turned[(c,) + here]
        u.append(value - jnp.sum(value, axis=0, keepdims=True) * (1.0 / LEAF))
    return u


def blocks_of(rows):
    for half in range(2):
        for block in range(rows // LANES):
            yield half, (slice(half * LEAF, (half + 1) * LEAF), slice(block * LANES, (block + 1) * LANES))


def list_groups(counts, batches, size, groups):
    def one(n, place):
        for i in range(size // ROWS):
            groups[place + i] = n * size + i * ROWS
        return place + (counts[n] + ROWS - 1) // ROWS

    return lax.fori_loop(0, batches, one, 0)


def each_group(groups, number, step):
    def several(turn, carry):
        step([groups[turn * JOINT + i] for i in range(JOINT)])
        return carry

    def single(turn, carry):
        step([groups[turn]])
        return carry

    lax.fori_loop(0, number // JOINT, several, 0)
    lax.fori_loop(number // JOINT * JOINT, number, single, 0)


def views(index, width):
    return [index.at[pl.ds(i, index.shape[0] - width + 1)] for i in range(width)]


def gather_rows(groups, number, index, table, held):
    later = views(index, ROWS)

    def step(firsts):
        for first in firsts:
            rows = [table[pl.ds(later[i][first], 1), :] for i in range(ROWS)]
            for i in range(ROWS):
                held[pl.ds(first + i, 1), :] = rows[i]

    each_group(groups, number, step)


def scatter_rows(groups, number, index, held, totals):
    for total in totals:
        total[...] = jnp.zeros_like(total)

    later = views(index, ROWS)

    def step(firsts):
        for first in firsts:
            for i in range(ROWS):
                total = totals[i % len(totals)]
                there = pl.ds(later[i][first], 1)
                total[there, :] = total[there, :] + held[pl.ds(first + i, 1), :]

    each_group(groups, number, step)


def sum_of(totals):
    return functools.reduce(lambda a, b: a + b, [total[...] for total in totals])


def dot(a, b):
    return jnp.dot(a, b, preferred_element_type=jnp.float32)


def multiply(value, both):
    high, low = split(value)
    return dot(high, both[:LANES]) + dot(low, both[:LANES]) + dot(high, both[LANES:])


def front_kernel(
    slots, classes, counts, targets, sources, signs, pos, mass, operators,
    message, packed,
    turned, terms, table, rows, matrix, both, held, *rest,
):
    *totals, groups, row_sem, out_sem = rest
    batches = rows.shape[0]
    size = held.shape[0] // batches
    leaf_rows = mass.shape[0]

    def fetch(n):
        return pltpu.make_async_copy(operators.at[pl.ds(classes[n], 1), :], rows.at[pl.ds(n, 1), :], row_sem)

    lax.fori_loop(0, batches, lambda n, c: (fetch(n).start(), c)[1], 0)
    for c in range(3):
        turned[c] = pos[c].T
    turned[3] = mass[...].T
    terms[...] = jnp.zeros_like(terms)
    for half, here in blocks_of(leaf_rows):

        def visit(k, value, half=half, here=here):
            terms[half, k : k + 1, here[1]] = jnp.sum(value, axis=0, keepdims=True)

        walk(*centred(turned, here), turned[(3,) + here], visit)
    for half in range(2):
        table[pl.ds(half, leaf_rows, 2), :] = terms[half].T
    cap = message.shape[1] // 2

    later = views(slots, ROWS)

    def export(group, carry):
        values = [table[pl.ds(later[i][group * ROWS], 1), :] for i in range(ROWS)]
        for i in range(ROWS):
            message[group * (ROWS // cap) + i // cap, i % cap : i % cap + 1, :] = values[i]
        return carry

    lax.fori_loop(0, slots.shape[0] // ROWS, export, 0)
    number = list_groups(counts, batches, size, groups)
    gather_rows(groups, number, targets, table, held)
    lax.fori_loop(0, batches, lambda n, c: (fetch(n).wait(), c)[1], 0)
    lane = lane_id((GROUP, LANES))
    width = rows.shape[1]
    matrix[:, COEFFS:, :] = jnp.zeros((batches, LANES - COEFFS, LANES), jnp.float32)

    def spread(group, carry):
        here = pl.ds(pl.multiple_of(group * GROUP, GROUP), GROUP)

        def part(first):
            value = rows[here, first * LANES : min((first + 1) * LANES, width)]
            if value.shape[1] < LANES:
                value = jnp.concatenate([value, jnp.zeros((GROUP, LANES - value.shape[1]), jnp.float32)], axis=1)
            return value

        for k in range(COEFFS):
            first, offset = divmod(k * COEFFS, LANES)
            value = part(first)
            if offset + COEFFS > LANES:
                value = jnp.where(lane < offset, part(first + 1), value)
            if offset:
                value = pltpu.roll(value, LANES - offset, 1)
            matrix[here, k, :] = jnp.where(lane < COEFFS, value, 0.0)
        return carry

    lax.fori_loop(0, batches // GROUP, spread, 0)
    row = lax.broadcasted_iota(jnp.int32, (size, LANES), 0)

    def product(n, carry):
        here = pl.ds(pl.multiple_of(n * size, size), size)
        value = jnp.where(row < counts[n], held[here, :], 0.0) * signs[...]
        high, low = split(matrix[n].T)
        both[n, :LANES] = high
        both[n, LANES:] = low
        held[here, :] = multiply(value, jnp.concatenate([high, low], axis=0))
        return carry

    lax.fori_loop(0, batches, product, 0, unroll=8)
    save = pltpu.make_async_copy(both, packed, out_sem)
    save.start()
    scatter_rows(groups, number, sources, held, totals)
    message[:, cap:, :] = (sum_of(totals) * signs[...]).reshape(message.shape[0], cap, LANES)
    save.wait()


def near_kernel(targets, sources, count, pos, mass, before, after, out, extended, lines, choose, ahead, source, target, total):
    rows = mass.shape[0]
    wide = lane_id((rows, LANES))
    for c in range(4):
        own = pos[c] if c < 3 else mass[...]
        extended[c, rows : extended.shape[1], :] = jnp.zeros((extended.shape[1] - rows, LANES), jnp.float32)
        extended[c, 1 : rows + 1, :] = own
        extended[c, 0:1, :] = before[c : c + 1, :]
        extended[c, rows + 1 : rows + 2, :] = after[c : c + 1, :]
        if c < 3:
            swapped = pltpu.roll(own, LEAF, 1)
            ahead[c, pl.ds(0, rows, 2), :] = jnp.where(wide < LEAF, own, swapped)
            ahead[c, pl.ds(1, rows, 2), :] = jnp.where(wide < LEAF, swapped, own)
    k_id = lax.broadcasted_iota(jnp.int32, (2 * LANES, 2 * LANES), 0)
    n_id = lax.broadcasted_iota(jnp.int32, (2 * LANES, 2 * LANES), 1)
    k_in = k_id % LANES
    code = (k_in // (3 * GROUP)) * GROUP + k_in % GROUP - n_id // LANES * GROUP
    code = jnp.where(k_id // LANES == n_id % LANES // LEAF, code, -1)
    tiles = choose.shape[0]

    def make_choice(tile, carry):
        wanted = tile // GROUP * 2 * GROUP + tile % GROUP
        choose[tile] = (code == wanted).astype(jnp.float32).astype(jnp.bfloat16)
        return carry

    lax.fori_loop(0, tiles, make_choice, 0)
    blocks = lines.shape[0] // LEAF
    for block in range(blocks):
        parts = []
        for c in range(4):
            value = extended[c, block * GROUP : (block + 1) * GROUP, :]
            for _ in range(2):
                high = value.astype(jnp.bfloat16).astype(jnp.float32)
                parts.append(high)
                value = value - high
            parts.append(value)
        parts.append(jnp.zeros((LANES - 12 * GROUP, LANES), jnp.float32))
        turned = jnp.concatenate(parts, axis=0).T.astype(jnp.bfloat16)
        quarter = LEAF // 2
        for parity in range(2):
            there = slice(block * LEAF + parity * quarter, block * LEAF + (parity + 1) * quarter)
            lines[there, :LANES] = turned[parity * LEAF : parity * LEAF + quarter]
            lines[there, LANES:] = turned[parity * LEAF + quarter : (parity + 1) * LEAF]
    share = blocks // 3

    def spread(step, carry):
        tile, third = step % tiles, step // tiles
        pair_of, r = tile // GROUP, tile % GROUP
        size = share * LEAF
        some = lines[pl.ds(pl.multiple_of(third * size, size), size), :]
        wide = jnp.dot(some, choose[tile], preferred_element_type=jnp.float32)
        for i in range(share):
            for parity in range(2):
                for q in range(4):
                    first = i * LEAF + parity * 32 + q * GROUP
                    leaf = 2 * ((third * share + i) * GROUP + r) + parity
                    for c in range(2):
                        source[leaf, (2 * pair_of + c) * 4 + q] = wide[first : first + GROUP, c * LANES : (c + 1) * LANES]
        return carry

    lax.fori_loop(0, 3 * tiles, spread, 0, unroll=2)

    def spread_target(leaf, carry):
        for c in range(3):
            target[leaf, c] = jnp.broadcast_to(ahead[c, pl.ds(leaf, 1), :], (GROUP, LANES))
        return carry

    lax.fori_loop(0, 2 * rows, spread_target, 0, unroll=4)
    total[...] = jnp.zeros_like(total)

    def pair(here, there):
        x, y, z = target[here, 0], target[here, 1], target[here, 2]
        parts = []
        for q in range(4):
            dx = x - source[there, q]
            dy = y - source[there, 4 + q]
            dz = z - source[there, 8 + q]
            distance = dx * dx + dy * dy + dz * dz
            inverse = jnp.where(distance > 0.0, lax.rsqrt(distance + SOFTENING), 0.0)
            parts.append(inverse * source[there, 12 + q])
        return here, (parts[0] + parts[1]) + (parts[2] + parts[3])

    later_target, later_source = views(targets, PAIRS), views(sources, PAIRS)

    def several(group, carry):
        first = group * PAIRS
        done = [pair(later_target[i][first], later_source[i][first]) for i in range(PAIRS)]
        for here, value in done:
            total[here] = total[here] + value
        return carry

    def single(j, carry):
        here, value = pair(targets[j], sources[j])
        total[here] = total[here] + value
        return carry

    live = count[0]
    full = live // PAIRS
    lax.fori_loop(0, full, several, 0)
    lax.fori_loop(full * PAIRS, live, single, 0)
    summed = jnp.sum(total[...], axis=1)
    ahead[0] = summed + pltpu.roll(summed, LEAF, 1)
    out[...] = -jnp.where(wide < LEAF, ahead[0, pl.ds(0, rows, 2), :], ahead[0, pl.ds(1, rows, 2), :])


def back_kernel(
    counts, sources, targets, slots, pos, near, packed, message,
    out,
    table, returned, both, held, expansion, turned, terms, *rest,
):
    *totals, groups, matrix_sem, table_sem, returned_sem = rest
    cap = table.shape[1]
    batches = both.shape[0]
    size = held.shape[0] // batches
    rows = near.shape[0]
    fetch_table = pltpu.make_async_copy(message.at[:, :cap, :], table, table_sem)
    fetch_table.start()
    fetch_returned = pltpu.make_async_copy(message.at[:, cap:, :], returned, returned_sem)
    fetch_returned.start()
    fetch_matrix = pltpu.make_async_copy(packed, both, matrix_sem)
    fetch_matrix.start()
    for c in range(3):
        turned[c] = pos[c].T
    number = list_groups(counts, batches, size, groups)
    fetch_table.wait()
    gather_rows(groups, number, sources, table.reshape(table.shape[0] * cap, LANES), held)
    fetch_matrix.wait()
    row = lax.broadcasted_iota(jnp.int32, (size, LANES), 0)

    def product(n, carry):
        here = pl.ds(pl.multiple_of(n * size, size), size)
        held[here, :] = multiply(jnp.where(row < counts[n], held[here, :], 0.0), both[n])
        return carry

    lax.fori_loop(0, batches, product, 0, unroll=8)
    scatter_rows(groups, number, targets, held, totals)
    fetch_returned.wait()
    chunk = slots.shape[1]
    leaf = lax.broadcasted_iota(jnp.int32, (expansion.shape[0], chunk), 0)
    sums = sum_of(totals)
    for block in range(slots.shape[0]):
        hot = (leaf == slots[block : block + 1, :]).astype(jnp.float32).astype(jnp.bfloat16)
        part = returned[block * chunk // cap : (block + 1) * chunk // cap]
        high, low = split(part.reshape(chunk, LANES))
        sums = sums + jnp.dot(hot, high, preferred_element_type=jnp.float32)
        sums = sums + jnp.dot(hot, low, preferred_element_type=jnp.float32)
    expansion[...] = sums
    for half in range(2):
        terms[half] = expansion[pl.ds(half, rows, 2), :].T
    for half, here in blocks_of(rows):
        sums = [jnp.zeros((LEAF, LANES), jnp.float32)]

        def visit(k, value, half=half, here=here, sums=sums):
            sums[0] = sums[0] + value * terms[half, k : k + 1, here[1]]

        walk(*centred(turned, here), jnp.ones((LEAF, LANES), jnp.float32), visit)
        turned[(3,) + here] = sums[0]
    out[...] = near[...] + turned[3].T


VMEM = pl.BlockSpec(memory_space=pltpu.VMEM)
SMEM = pl.BlockSpec(memory_space=pltpu.SMEM)
ANY = pl.BlockSpec(memory_space=pl.ANY)


def shape(*dims):
    return jax.ShapeDtypeStruct(dims, jnp.float32)


def params(mib):
    return pltpu.CompilerParams(vmem_limit_bytes=mib * MIB)


def scratch(*dims, dtype=jnp.float32):
    return pltpu.VMEM(dims, dtype)


def group_list(pairs, batches):
    return pltpu.SMEM((pairs // ROWS + pairs // batches // ROWS,), jnp.int32)


def front(slots, classes, counts, targets, sources, pos, mass, operators, devices):
    rows = mass.shape[0]
    batches, pairs = classes.shape[0], targets.shape[0]
    return pl.pallas_call(
        front_kernel,
        out_shape=(
            shape(devices, 2 * slots.shape[0] // devices, LANES),
            jax.ShapeDtypeStruct((batches, 2 * LANES, LANES), jnp.bfloat16),
        ),
        in_specs=[SMEM] * 5 + [VMEM] * 3 + [ANY],
        out_specs=(VMEM, ANY),
        scratch_shapes=[
            scratch(4, LANES, rows),
            scratch(2, LANES, rows),
            scratch(2 * rows, LANES),
            scratch(batches, operators.shape[1]),
            scratch(batches, LANES, LANES),
            scratch(batches, 2 * LANES, LANES, dtype=jnp.bfloat16),
            scratch(pairs, LANES),
        ]
        + [scratch(slots.shape[0], LANES)] * ACCS
        + [group_list(pairs, batches)]
        + [pltpu.SemaphoreType.DMA] * 2,
        compiler_params=params(58),
        name="front",
    )(slots, classes, counts, targets, sources, jnp.asarray(SIGNS), pos, mass, operators)


def back(counts, sources, targets, slots, pos, near, packed, message):
    rows = near.shape[0]
    cap = message.shape[1] // 2
    return pl.pallas_call(
        back_kernel,
        out_shape=shape(rows, LANES),
        in_specs=[SMEM] * 3 + [VMEM] * 3 + [ANY] * 2,
        out_specs=VMEM,
        scratch_shapes=[
            scratch(message.shape[0], cap, LANES),
            scratch(message.shape[0], cap, LANES),
            scratch(*packed.shape, dtype=jnp.bfloat16),
            scratch(sources.shape[0], LANES),
            scratch(2 * rows, LANES),
            scratch(4, LANES, rows),
            scratch(2, LANES, rows),
        ]
        + [scratch(2 * rows, LANES)] * ACCS
        + [group_list(sources.shape[0], counts.shape[0])]
        + [pltpu.SemaphoreType.DMA] * 3,
        compiler_params=params(58),
        name="back",
    )(counts, sources, targets, slots, pos, near, packed, message)


def near_field(targets, sources, count, pos, mass, before, after):
    rows = mass.shape[0]
    blocks = -(-(rows + 2) // (3 * GROUP)) * 3
    return pl.pallas_call(
        near_kernel,
        out_shape=shape(rows, LANES),
        in_specs=[SMEM] * 3 + [VMEM] * 4,
        out_specs=VMEM,
        scratch_shapes=[
            scratch(4, blocks * GROUP, LANES),
            scratch(blocks * LEAF, 2 * LANES, dtype=jnp.bfloat16),
            scratch(2 * GROUP, 2 * LANES, 2 * LANES, dtype=jnp.bfloat16),
            scratch(3, 2 * rows, LANES),
            scratch(2 * blocks * GROUP, 16, GROUP, LANES),
            scratch(2 * rows, 3, GROUP, LANES),
            scratch(2 * rows, GROUP, LANES),
        ],
        compiler_params=params(58),
        name="near_field",
    )(targets, sources, count, pos, mass, before, after)


AXES = ("group", "dom")


def exchange(value):
    return lax.all_to_all(value, AXES, split_axis=0, concat_axis=0, tiled=True)


def shift(value, forward):
    count = lax.axis_size("group") * lax.axis_size("dom")
    pairs = [(i, i + 1) for i in range(count - 1)] if forward else [(i + 1, i) for i in range(count - 1)]
    return lax.ppermute(value, AXES, pairs)


def local(
    positions,
    masses,
    near_target,
    near_source,
    near_count,
    far_target,
    far_source,
    far_class,
    far_count,
    export_slots,
    operators,
):
    devices = lax.axis_size("group") * lax.axis_size("dom")
    slots = export_slots.reshape(-1)
    pos = positions.reshape(3, -1, LANES)
    mass = masses.reshape(-1, LANES)
    ends = jnp.concatenate([pos[:, :: mass.shape[0] - 1], mass[None, :: mass.shape[0] - 1]], axis=0)
    before = shift(ends[:, 1], True)
    after = shift(ends[:, 0], False)
    message, packed = front(slots, far_class, far_count, far_target, far_source, pos, mass, operators, devices)
    message, before, after = lax.optimization_barrier((message, before, after))
    message = exchange(message)
    near = near_field(near_target, near_source, near_count, pos, mass, before, after)
    out = back(far_count, far_source, far_target, slots.reshape(8, -1), pos, near, packed, message)
    return out.reshape(-1)


def solution(mesh):
    split_all = P(AXES)
    in_specs = (P(None, AXES),) + (split_all,) * 8 + (P(AXES, None), P())
    return jax.shard_map(local, mesh=mesh, in_specs=in_specs, out_specs=split_all, check_vma=False)
```

```python
import functools

import jax
import jax.numpy as jnp
import numpy as np
from jax import lax
from jax.experimental import pallas as pl
from jax.experimental.pallas import tpu as pltpu
from jax.sharding import PartitionSpec as P

LEAF = 64
ORDER = 6
LANES = 128
SOFTENING = 0.01
ACCS = 8
GROUP = 8
ROWS = 16
PAIRS = 32
JOINT = 8
BESIDE = 32
CAP = 8
ROW_COUNT = 11
SPARE = ROW_COUNT - CAP
MIB = 1 << 20


def exponent_table(degree_max):
    triples = []
    for degree in range(degree_max + 1):
        for first_pow in range(degree, -1, -1):
            for second_pow in range(degree - first_pow, -1, -1):
                triples.append((first_pow, second_pow, degree - first_pow - second_pow))
    return triples


TRIPLES = exponent_table(ORDER)
COEFFS = len(TRIPLES)
INDEX = {triple: k for k, triple in enumerate(TRIPLES)}
SIGNS = np.ones((1, LANES), np.float32)
SIGNS[0, :COEFFS] = [(-1.0) ** sum(triple) for triple in TRIPLES]


def split(value):
    high = value.astype(jnp.bfloat16)
    return high, (value - high.astype(jnp.float32)).astype(jnp.bfloat16)


def lane_id(shape):
    return lax.broadcasted_iota(jnp.int32, shape, len(shape) - 1)


def walk(x, y, z, start, visit):
    along_x = start
    for a in range(ORDER + 1):
        along_y = along_x
        for b in range(ORDER + 1 - a):
            along_z = along_y
            for c in range(ORDER + 1 - a - b):
                visit(INDEX[(a, b, c)], along_z)
                if c < ORDER - a - b:
                    along_z = along_z * z
            if b < ORDER - a:
                along_y = along_y * y
        if a < ORDER:
            along_x = along_x * x


def sum_sublanes(value, count):
    return functools.reduce(lambda a, b: a + b, [value[pl.ds(i, count, GROUP), :] for i in range(GROUP)])


def centred(turned, here):
    u = []
    for c in range(3):
        value = turned[(c,) + here]
        u.append(value - jnp.sum(value, axis=0, keepdims=True) * (1.0 / LEAF))
    return u


def block_of(here):
    return here[1].start // LANES


def blocks_of(rows):
    for half in range(2):
        for block in range(rows // LANES):
            yield half, (slice(half * LEAF, (half + 1) * LEAF), slice(block * LANES, (block + 1) * LANES))


def list_groups(counts, batches, size, groups):
    def one(n, place):
        for i in range(size // ROWS):
            groups[place + i] = n * size + i * ROWS
        return place + (counts[n] + ROWS - 1) // ROWS

    return lax.fori_loop(0, batches, one, 0, unroll=4)


def each_group(groups, start, number, step):
    def several(turn, carry):
        step([groups[turn * JOINT + i] for i in range(JOINT)])
        return carry

    def single(turn, carry):
        step([groups[turn]])
        return carry

    lax.fori_loop(start // JOINT, number // JOINT, several, 0)
    lax.fori_loop(jnp.maximum(number // JOINT * JOINT, start), number, single, 0)


def views(index, width):
    return [index.at[pl.ds(i, index.shape[0] - width + 1)] for i in range(width)]


def gather_step(index, table, held):
    later = views(index, ROWS)

    def step(firsts):
        for first in firsts:
            rows = [table[pl.ds(later[i][first], 1), :] for i in range(ROWS)]
            for i in range(ROWS):
                held[pl.ds(first + i, 1), :] = rows[i]

    return step


def scatter_rows(groups, number, index, held, totals):
    for total in totals:
        total[...] = jnp.zeros_like(total)

    later = views(index, ROWS)

    def step(firsts):
        for first in firsts:
            for i in range(ROWS):
                total = totals[i % len(totals)]
                there = pl.ds(later[i][first], 1)
                total[there, :] = total[there, :] + held[pl.ds(first + i, 1), :]

    each_group(groups, 0, number, step)


def sum_of(totals):
    return functools.reduce(lambda a, b: a + b, [total[...] for total in totals])


def dot(a, b):
    return jnp.dot(a, b, preferred_element_type=jnp.float32)


def multiply(value, both):
    high, low = split(value)
    return dot(high, both[:LANES]) + dot(low, both[:LANES]) + dot(high, both[LANES:])


def front_kernel(
    slots, classes, counts, signs, pos, mass, operators, all_targets, all_sources,
    message, groups, packed,
    turned, terms, parts, table, rows, matrix, both, held, targets, sources, *rest,
):
    *totals, row_sem, out_sem, target_sem, source_sem = rest
    batches = rows.shape[0]
    size = held.shape[0] // batches
    leaf_rows = mass.shape[0]

    fetch_targets = pltpu.make_async_copy(all_targets, targets, target_sem)
    fetch_targets.start()
    fetch_sources = pltpu.make_async_copy(all_sources, sources, source_sem)
    fetch_sources.start()

    def fetch(n):
        return pltpu.make_async_copy(operators.at[pl.ds(classes[n], 1), :], rows.at[pl.ds(n, 1), :], row_sem)

    lax.fori_loop(0, batches, lambda n, c: (fetch(n).start(), c)[1], 0, unroll=8)
    for c in range(3):
        turned[c] = pos[c].T
    turned[3] = mass[...].T
    terms[...] = jnp.zeros_like(terms)
    for half, here in blocks_of(leaf_rows):

        def visit(k, value, half=half, here=here):
            whole = functools.reduce(lambda a, b: a + b, [value[i : i + GROUP] for i in range(0, LEAF, GROUP)])
            parts[half, block_of(here), k * GROUP : (k + 1) * GROUP, :] = whole

        walk(*centred(turned, here), turned[(3,) + here], visit)
    for half in range(2):
        for block in range(leaf_rows // LANES):
            terms[half, :COEFFS, block * LANES : (block + 1) * LANES] = sum_sublanes(parts.at[half, block], COEFFS)
        table[pl.ds(half, leaf_rows, 2), :] = terms[half].T
    devices = message.shape[0] // ROW_COUNT
    later = views(slots, ROWS)

    def export(group, carry):
        values = [table[pl.ds(later[i][group * ROWS], 1), :] for i in range(ROWS)]
        for i in range(ROWS):
            message[pl.ds(group * (ROWS // CAP * ROW_COUNT) + i // CAP * ROW_COUNT + i % CAP, 1), :] = values[i]
        return carry

    lax.fori_loop(0, slots.shape[0] // ROWS, export, 0, unroll=4)
    number = list_groups(counts, batches, size, groups)
    groups[groups.shape[0] - 1] = number
    fetch_targets.wait()
    gather = gather_step(targets, table, held)
    beside = BESIDE * batches // GROUP

    def fill(place, carry):
        groups[place] = 0
        return carry

    lax.fori_loop(number, beside, fill, 0)
    lax.fori_loop(0, batches, lambda n, c: (fetch(n).wait(), c)[1], 0, unroll=8)
    lane = lane_id((GROUP, LANES))
    width = rows.shape[1]
    flat = matrix.reshape(batches * LANES, LANES)
    matrix[:, COEFFS:, :] = jnp.zeros((batches, LANES - COEFFS, LANES), jnp.float32)

    def spread(group, carry):
        here = pl.ds(pl.multiple_of(group * GROUP, GROUP), GROUP)

        def part(first):
            value = rows[here, first * LANES : min((first + 1) * LANES, width)]
            if value.shape[1] < LANES:
                value = jnp.concatenate([value, jnp.zeros((GROUP, LANES - value.shape[1]), jnp.float32)], axis=1)
            return value

        for k in range(COEFFS):
            first, offset = divmod(k * COEFFS, LANES)
            value = part(first)
            if offset + COEFFS > LANES:
                value = jnp.where(lane < offset, part(first + 1), value)
            if offset:
                value = pltpu.roll(value, LANES - offset, 1)
            flat[pl.ds(group * GROUP * LANES + k, GROUP, LANES), :] = jnp.where(lane < COEFFS, value, 0.0)
            if k * BESIDE // COEFFS < (k + 1) * BESIDE // COEFFS:
                gather([groups[group * BESIDE + k * BESIDE // COEFFS]])
        return carry

    lax.fori_loop(0, batches // GROUP, spread, 0)
    each_group(groups, beside, number, gather)
    row = lax.broadcasted_iota(jnp.int32, (size, LANES), 0)

    def product(n, carry):
        here = pl.ds(pl.multiple_of(n * size, size), size)
        value = jnp.where(row < counts[n], held[here, :], 0.0) * signs[...]
        high, low = split(matrix[n].T)
        both[n, :LANES] = high
        both[n, LANES:] = low
        held[here, :] = multiply(value, jnp.concatenate([high, low], axis=0))
        return carry

    lax.fori_loop(0, batches, product, 0, unroll=8)
    save = pltpu.make_async_copy(both, packed, out_sem)
    save.start()
    fetch_sources.wait()
    scatter_rows(groups, number, sources, held, totals)
    totals[0][...] = sum_of(totals) * signs[...]
    every = lane_id((devices, LANES))
    holes = []
    for c in range(CAP):
        value = totals[0][pl.ds(c, devices, CAP), :]
        if c < SPARE:
            holes.append((CAP + c, value))
        else:
            first = 2 * (c - SPARE)
            holes.append((first, jnp.where(every < COEFFS, 0.0, pltpu.roll(value, COEFFS, 1))))
            holes.append((first + 1, jnp.where(every < COEFFS, 0.0, pltpu.roll(value, 2 * COEFFS - LANES, 1))))
    for r in range(ROW_COUNT):
        value = sum([v for place, v in holes if place == r], 0.0)
        there = pl.ds(r, devices, ROW_COUNT)
        message[there, :] = value if r >= CAP else message[there, :] + value
    save.wait()


def near_kernel(targets, sources, count, pos, mass, before, after, out, extended, lines, choose, ahead, source, target, total):
    rows = mass.shape[0]
    wide = lane_id((rows, LANES))
    for c in range(4):
        own = pos[c] if c < 3 else mass[...]
        extended[c, rows : extended.shape[1], :] = jnp.zeros((extended.shape[1] - rows, LANES), jnp.float32)
        extended[c, 1 : rows + 1, :] = own
        extended[c, 0:1, :] = before[c : c + 1, :]
        extended[c, rows + 1 : rows + 2, :] = after[c : c + 1, :]
        if c < 3:
            swapped = pltpu.roll(own, LEAF, 1)
            ahead[c, pl.ds(0, rows, 2), :] = jnp.where(wide < LEAF, own, swapped)
            ahead[c, pl.ds(1, rows, 2), :] = jnp.where(wide < LEAF, swapped, own)
    k_id = lax.broadcasted_iota(jnp.int32, (2 * LANES, 2 * LANES), 0)
    n_id = lax.broadcasted_iota(jnp.int32, (2 * LANES, 2 * LANES), 1)
    k_in = k_id % LANES
    code = (k_in // (3 * GROUP)) * GROUP + k_in % GROUP - n_id // LANES * GROUP
    code = jnp.where(k_id // LANES == n_id % LANES // LEAF, code, -1)
    tiles = choose.shape[0]

    def make_choice(tile, carry):
        wanted = tile // GROUP * 2 * GROUP + tile % GROUP
        choose[tile] = (code == wanted).astype(jnp.float32).astype(jnp.bfloat16)
        return carry

    lax.fori_loop(0, tiles, make_choice, 0)
    blocks = lines.shape[0] // LEAF
    for block in range(blocks):
        parts = []
        for c in range(4):
            value = extended[c, block * GROUP : (block + 1) * GROUP, :]
            for _ in range(2):
                high = value.astype(jnp.bfloat16).astype(jnp.float32)
                parts.append(high)
                value = value - high
            parts.append(value)
        parts.append(jnp.zeros((LANES - 12 * GROUP, LANES), jnp.float32))
        turned = jnp.concatenate(parts, axis=0).T.astype(jnp.bfloat16)
        quarter = LEAF // 2
        for parity in range(2):
            there = slice(block * LEAF + parity * quarter, block * LEAF + (parity + 1) * quarter)
            lines[there, :LANES] = turned[parity * LEAF : parity * LEAF + quarter]
            lines[there, LANES:] = turned[parity * LEAF + quarter : (parity + 1) * LEAF]
    share = blocks // 3

    def spread(step, carry):
        tile, third = step % tiles, step // tiles
        pair_of, r = tile // GROUP, tile % GROUP
        size = share * LEAF
        some = lines[pl.ds(pl.multiple_of(third * size, size), size), :]
        wide = jnp.dot(some, choose[tile], preferred_element_type=jnp.float32)
        for i in range(share):
            for parity in range(2):
                for q in range(4):
                    first = i * LEAF + parity * 32 + q * GROUP
                    leaf = 2 * ((third * share + i) * GROUP + r) + parity
                    for c in range(2):
                        source[leaf, (2 * pair_of + c) * 4 + q] = wide[first : first + GROUP, c * LANES : (c + 1) * LANES]
        return carry

    lax.fori_loop(0, 3 * tiles, spread, 0, unroll=4)

    def spread_target(leaf, carry):
        for c in range(3):
            target[leaf, c] = jnp.broadcast_to(ahead[c, pl.ds(leaf, 1), :], (GROUP, LANES))
        return carry

    lax.fori_loop(0, 2 * rows, spread_target, 0, unroll=4)
    total[...] = jnp.zeros_like(total)

    def pair(here, there):
        x, y, z = target[here, 0], target[here, 1], target[here, 2]
        parts = []
        for q in range(4):
            dx = x - source[there, q]
            dy = y - source[there, 4 + q]
            dz = z - source[there, 8 + q]
            distance = dx * dx + dy * dy + dz * dz
            inverse = jnp.where(distance > 0.0, lax.rsqrt(distance + SOFTENING), 0.0)
            parts.append(inverse * source[there, 12 + q])
        return here, (parts[0] + parts[1]) + (parts[2] + parts[3])

    later_target, later_source = views(targets, PAIRS), views(sources, PAIRS)

    def several(group, carry):
        first = group * PAIRS
        done = [pair(later_target[i][first], later_source[i][first]) for i in range(PAIRS)]
        for here, value in done:
            total[here] = total[here] + value
        return carry

    def single(j, carry):
        here, value = pair(targets[j], sources[j])
        total[here] = total[here] + value
        return carry

    live = count[0]
    full = live // PAIRS
    lax.fori_loop(0, full, several, 0)
    lax.fori_loop(full * PAIRS, live, single, 0)
    summed = sum_sublanes(total.reshape(2 * rows * GROUP, LANES), 2 * rows)
    ahead[0] = summed + pltpu.roll(summed, LEAF, 1)
    out[...] = -jnp.where(wide < LEAF, ahead[0, pl.ds(0, rows, 2), :], ahead[0, pl.ds(1, rows, 2), :])


def back_kernel(
    counts, groups, slots, pos, near, packed, message, all_sources, all_targets,
    out,
    rows_in, table, returned, both, held, expansion, turned, terms, sources, targets, *rest,
):
    *totals, matrix_sem, message_sem, source_sem, target_sem = rest
    batches = both.shape[0]
    size = held.shape[0] // batches
    rows = near.shape[0]
    fetch_sources = pltpu.make_async_copy(all_sources, sources, source_sem)
    fetch_sources.start()
    fetch_message = pltpu.make_async_copy(message, rows_in, message_sem)
    fetch_message.start()
    fetch_targets = pltpu.make_async_copy(all_targets, targets, target_sem)
    fetch_targets.start()
    fetch_matrix = pltpu.make_async_copy(packed, both, matrix_sem)
    fetch_matrix.start()
    for c in range(3):
        turned[c] = pos[c].T
    number = groups[groups.shape[0] - 1]
    devices = rows_in.shape[0] // ROW_COUNT
    every = lane_id((devices, LANES))
    fetch_message.wait()

    def received(r):
        return rows_in[pl.ds(r, devices, ROW_COUNT), :]

    for c in range(CAP):
        table[pl.ds(c, devices, CAP), :] = received(c)
        if c < SPARE:
            value = received(CAP + c)
        else:
            first = 2 * (c - SPARE)
            early = pltpu.roll(received(first), LANES - COEFFS, 1)
            late = pltpu.roll(received(first + 1), 2 * (LANES - COEFFS), 1)
            value = jnp.where(every < LANES - COEFFS, early, late)
        returned[pl.ds(c, devices, CAP), :] = value
    fetch_sources.wait()
    each_group(groups, 0, number, gather_step(sources, table, held))
    fetch_matrix.wait()
    row = lax.broadcasted_iota(jnp.int32, (size, LANES), 0)

    def product(n, carry):
        here = pl.ds(pl.multiple_of(n * size, size), size)
        held[here, :] = multiply(jnp.where(row < counts[n], held[here, :], 0.0), both[n])
        return carry

    lax.fori_loop(0, batches, product, 0, unroll=8)
    fetch_targets.wait()
    scatter_rows(groups, number, targets, held, totals)
    chunk = slots.shape[1]
    leaf = lax.broadcasted_iota(jnp.int32, (expansion.shape[0], chunk), 0)
    sums = sum_of(totals)
    for block in range(slots.shape[0]):
        hot = (leaf == slots[block : block + 1, :]).astype(jnp.float32).astype(jnp.bfloat16)
        high, low = split(returned[block * chunk : (block + 1) * chunk, :])
        sums = sums + jnp.dot(hot, high, preferred_element_type=jnp.float32)
        sums = sums + jnp.dot(hot, low, preferred_element_type=jnp.float32)
    expansion[...] = sums
    for half in range(2):
        terms[half] = expansion[pl.ds(half, rows, 2), :].T
    for half, here in blocks_of(rows):
        sums = [jnp.zeros((LEAF, LANES), jnp.float32)]

        def visit(k, value, half=half, here=here, sums=sums):
            sums[0] = sums[0] + value * terms[half, k : k + 1, here[1]]

        walk(*centred(turned, here), jnp.ones((LEAF, LANES), jnp.float32), visit)
        turned[(3,) + here] = sums[0]
    out[...] = near[...] + turned[3].T


VMEM = pl.BlockSpec(memory_space=pltpu.VMEM)
SMEM = pl.BlockSpec(memory_space=pltpu.SMEM)
ANY = pl.BlockSpec(memory_space=pl.ANY)


def shape(*dims):
    return jax.ShapeDtypeStruct(dims, jnp.float32)


def params(mib):
    return pltpu.CompilerParams(vmem_limit_bytes=mib * MIB)


def scratch(*dims, dtype=jnp.float32):
    return pltpu.VMEM(dims, dtype)


def front(slots, classes, counts, targets, sources, pos, mass, operators, devices):
    rows = mass.shape[0]
    batches, pairs = classes.shape[0], targets.shape[0]
    most = pairs // ROWS + pairs // batches // ROWS + 1
    return pl.pallas_call(
        front_kernel,
        out_shape=(
            shape(devices * ROW_COUNT, LANES),
            jax.ShapeDtypeStruct((-(-most // 1024) * 1024,), jnp.int32),
            jax.ShapeDtypeStruct((batches, 2 * LANES, LANES), jnp.bfloat16),
        ),
        in_specs=[SMEM] * 3 + [VMEM] * 3 + [ANY] * 3,
        out_specs=(VMEM, SMEM, ANY),
        scratch_shapes=[
            scratch(4, LANES, rows),
            scratch(2, LANES, rows),
            scratch(2, rows // LANES, COEFFS * GROUP, LANES),
            scratch(2 * rows, LANES),
            scratch(batches, operators.shape[1]),
            scratch(batches, LANES, LANES),
            scratch(batches, 2 * LANES, LANES, dtype=jnp.bfloat16),
            scratch(pairs, LANES),
            pltpu.SMEM((pairs,), jnp.int32),
            pltpu.SMEM((pairs,), jnp.int32),
        ]
        + [scratch(slots.shape[0], LANES)] * ACCS
        + [pltpu.SemaphoreType.DMA] * 4,
        compiler_params=params(58),
        name="front",
    )(slots, classes, counts, jnp.asarray(SIGNS), pos, mass, operators, targets, sources)


def back(counts, groups, sources, targets, slots, pos, near, packed, message):
    rows = near.shape[0]
    pairs = sources.shape[0]
    return pl.pallas_call(
        back_kernel,
        out_shape=shape(rows, LANES),
        in_specs=[SMEM] * 2 + [VMEM] * 3 + [ANY] * 4,
        out_specs=VMEM,
        scratch_shapes=[
            scratch(*message.shape),
            scratch(slots.size, LANES),
            scratch(slots.size, LANES),
            scratch(*packed.shape, dtype=jnp.bfloat16),
            scratch(pairs, LANES),
            scratch(2 * rows, LANES),
            scratch(4, LANES, rows),
            scratch(2, LANES, rows),
            pltpu.SMEM((pairs,), jnp.int32),
            pltpu.SMEM((pairs,), jnp.int32),
        ]
        + [scratch(2 * rows, LANES)] * ACCS
        + [pltpu.SemaphoreType.DMA] * 4,
        compiler_params=params(58),
        name="back",
    )(counts, groups, slots, pos, near, packed, message, sources, targets)


def near_field(targets, sources, count, pos, mass, before, after):
    rows = mass.shape[0]
    blocks = -(-(rows + 2) // (3 * GROUP)) * 3
    return pl.pallas_call(
        near_kernel,
        out_shape=shape(rows, LANES),
        in_specs=[SMEM] * 3 + [VMEM] * 4,
        out_specs=VMEM,
        scratch_shapes=[
            scratch(4, blocks * GROUP, LANES),
            scratch(blocks * LEAF, 2 * LANES, dtype=jnp.bfloat16),
            scratch(2 * GROUP, 2 * LANES, 2 * LANES, dtype=jnp.bfloat16),
            scratch(3, 2 * rows, LANES),
            scratch(2 * blocks * GROUP, 16, GROUP, LANES),
            scratch(2 * rows, 3, GROUP, LANES),
            scratch(2 * rows, GROUP, LANES),
        ],
        compiler_params=params(58),
        name="near_field",
    )(targets, sources, count, pos, mass, before, after)


AXES = ("group", "dom")


def exchange(value):
    devices = lax.axis_size("group") * lax.axis_size("dom")
    blocks = value.reshape(devices, -1, 1, LANES)
    return lax.all_to_all(blocks, AXES, split_axis=0, concat_axis=0, tiled=True).reshape(value.shape)


def shift(value, forward):
    count = lax.axis_size("group") * lax.axis_size("dom")
    pairs = [(i, i + 1) for i in range(count - 1)] if forward else [(i + 1, i) for i in range(count - 1)]
    return lax.ppermute(value, AXES, pairs)


def local(
    positions,
    masses,
    near_target,
    near_source,
    near_count,
    far_target,
    far_source,
    far_class,
    far_count,
    export_slots,
    operators,
):
    devices = lax.axis_size("group") * lax.axis_size("dom")
    slots = export_slots.reshape(-1)
    pos = positions.reshape(3, -1, LANES)
    mass = masses.reshape(-1, LANES)
    ends = jnp.concatenate([pos[:, :: mass.shape[0] - 1], mass[None, :: mass.shape[0] - 1]], axis=0)
    before = shift(ends[:, 1], True)
    after = shift(ends[:, 0], False)
    message, groups, packed = front(slots, far_class, far_count, far_target, far_source, pos, mass, operators, devices)
    message, before, after = lax.optimization_barrier((message, before, after))
    message = exchange(message)
    near = near_field(near_target, near_source, near_count, pos, mass, before, after)
    out = back(far_count, groups, far_source, far_target, slots.reshape(8, -1), pos, near, packed, message)
    return out.reshape(-1)


def solution(mesh):
    split_all = P(AXES)
    in_specs = (P(None, AXES),) + (split_all,) * 8 + (P(AXES, None), P())
    return jax.shard_map(local, mesh=mesh, in_specs=in_specs, out_specs=split_all, check_vma=False)
```

```python
import functools

import jax
import jax.numpy as jnp
import numpy as np
from jax import lax
from jax.experimental import pallas as pl
from jax.experimental.pallas import tpu as pltpu
from jax.sharding import PartitionSpec as P

LEAF = 64
ORDER = 6
LANES = 128
SOFTENING = 0.01
ACCS = 8
GROUP = 8
ROWS = 16
PAIRS = 64
JOINT = 4
BESIDE = 32
CAP = 8
ROW_COUNT = 11
SPARE = ROW_COUNT - CAP
MIB = 1 << 20


def exponent_table(degree_max):
    triples = []
    for degree in range(degree_max + 1):
        for first_pow in range(degree, -1, -1):
            for second_pow in range(degree - first_pow, -1, -1):
                triples.append((first_pow, second_pow, degree - first_pow - second_pow))
    return triples


TRIPLES = exponent_table(ORDER)
COEFFS = len(TRIPLES)
INDEX = {triple: k for k, triple in enumerate(TRIPLES)}
SIGNS = np.ones((1, LANES), np.float32)
SIGNS[0, :COEFFS] = [(-1.0) ** sum(triple) for triple in TRIPLES]


def split(value):
    high = value.astype(jnp.bfloat16)
    return high, (value - high.astype(jnp.float32)).astype(jnp.bfloat16)


def lane_id(shape):
    return lax.broadcasted_iota(jnp.int32, shape, len(shape) - 1)


def walk(x, y, z, start, visit):
    along_x = start
    for a in range(ORDER + 1):
        along_y = along_x
        for b in range(ORDER + 1 - a):
            along_z = along_y
            for c in range(ORDER + 1 - a - b):
                visit(INDEX[(a, b, c)], along_z)
                if c < ORDER - a - b:
                    along_z = along_z * z
            if b < ORDER - a:
                along_y = along_y * y
        if a < ORDER:
            along_x = along_x * x


def sum_sublanes(value, count):
    return functools.reduce(lambda a, b: a + b, [value[pl.ds(i, count, GROUP), :] for i in range(GROUP)])


def centred(turned, here):
    u = []
    for c in range(3):
        value = turned[(c,) + here]
        u.append(value - jnp.sum(value, axis=0, keepdims=True) * (1.0 / LEAF))
    return u


def block_of(here):
    return here[1].start // LANES


def blocks_of(rows):
    for half in range(2):
        for block in range(rows // LANES):
            yield half, (slice(half * LEAF, (half + 1) * LEAF), slice(block * LANES, (block + 1) * LANES))


def list_groups(counts, batches, size, groups):
    share = size // ROWS
    later = [groups.at[pl.ds(i, groups.shape[0] - share + 1)] for i in range(share)]

    def one(n, place):
        for i in range(share):
            later[i][place] = n * size + i * ROWS
        return place + (counts[n] + ROWS - 1) // ROWS

    return lax.fori_loop(0, batches, one, 0, unroll=4)


def each_group(groups, start, number, step):
    def several(turn, carry):
        step([groups[turn * JOINT + i] for i in range(JOINT)])
        return carry

    def single(turn, carry):
        step([groups[turn]])
        return carry

    lax.fori_loop(start // JOINT, number // JOINT, several, 0)
    lax.fori_loop(jnp.maximum(number // JOINT * JOINT, start), number, single, 0)


def views(index, width):
    return [index.at[pl.ds(i, index.shape[0] - width + 1)] for i in range(width)]


def gather_step(index, table, held):
    later = views(index, ROWS)

    def step(firsts):
        for first in firsts:
            rows = [table[pl.ds(later[i][first], 1), :] for i in range(ROWS)]
            for i in range(ROWS):
                held[pl.ds(first + i, 1), :] = rows[i]

    return step


def scatter_rows(groups, number, index, held, totals):
    for total in totals:
        total[...] = jnp.zeros_like(total)

    later = views(index, ROWS)

    def step(firsts):
        for first in firsts:
            for i in range(ROWS):
                total = totals[i % len(totals)]
                there = pl.ds(later[i][first], 1)
                total[there, :] = total[there, :] + held[pl.ds(first + i, 1), :]

    each_group(groups, 0, number, step)


def sum_of(totals):
    return functools.reduce(lambda a, b: a + b, [total[...] for total in totals])


def dot(a, b):
    return jnp.dot(a, b, preferred_element_type=jnp.float32)


def multiply(value, both):
    high, low = split(value)
    return dot(high, both[:LANES]) + dot(low, both[:LANES]) + dot(high, both[LANES:])


def front_kernel(
    classes, counts, signs, pos, mass, operators, all_slots, all_targets, all_sources,
    message, groups, packed,
    turned, terms, parts, table, rows, matrix, both, held, slots, targets, sources, *rest,
):
    *totals, row_sem, out_sem, slot_sem, target_sem, source_sem = rest
    batches = rows.shape[0]
    size = held.shape[0] // batches
    leaf_rows = mass.shape[0]

    fetch_slots = pltpu.make_async_copy(all_slots, slots, slot_sem)
    fetch_slots.start()
    fetch_targets = pltpu.make_async_copy(all_targets, targets, target_sem)
    fetch_targets.start()
    fetch_sources = pltpu.make_async_copy(all_sources, sources, source_sem)
    fetch_sources.start()

    def fetch(n):
        return pltpu.make_async_copy(operators.at[pl.ds(classes[n], 1), :], rows.at[pl.ds(n, 1), :], row_sem)

    lax.fori_loop(0, batches, lambda n, c: (fetch(n).start(), c)[1], 0, unroll=8)
    for c in range(3):
        turned[c] = pos[c].T
    turned[3] = mass[...].T
    terms[...] = jnp.zeros_like(terms)
    for half, here in blocks_of(leaf_rows):

        def visit(k, value, half=half, here=here):
            whole = functools.reduce(lambda a, b: a + b, [value[i : i + GROUP] for i in range(0, LEAF, GROUP)])
            parts[half, block_of(here), k * GROUP : (k + 1) * GROUP, :] = whole

        walk(*centred(turned, here), turned[(3,) + here], visit)
    for half in range(2):
        for block in range(leaf_rows // LANES):
            terms[half, :COEFFS, block * LANES : (block + 1) * LANES] = sum_sublanes(parts.at[half, block], COEFFS)
        table[pl.ds(half, leaf_rows, 2), :] = terms[half].T
    devices = message.shape[0] // ROW_COUNT
    fetch_slots.wait()

    def export(device, carry):
        values = [table[pl.ds(slots[c, device], 1), :] for c in range(CAP)]
        for c in range(CAP):
            message[pl.ds(device * ROW_COUNT + c, 1), :] = values[c]
        return carry

    lax.fori_loop(0, devices, export, 0, unroll=8)
    number = list_groups(counts, batches, size, groups)
    groups[groups.shape[0] - 1] = number
    fetch_targets.wait()
    gather = gather_step(targets, table, held)
    beside = BESIDE * batches // GROUP

    def fill(place, carry):
        groups[place] = 0
        return carry

    lax.fori_loop(number, beside, fill, 0)
    lax.fori_loop(0, batches, lambda n, c: (fetch(n).wait(), c)[1], 0, unroll=8)
    lane = lane_id((GROUP, LANES))
    width = rows.shape[1]
    flat = matrix.reshape(batches * LANES, LANES)
    matrix[:, COEFFS:, :] = jnp.zeros((batches, LANES - COEFFS, LANES), jnp.float32)

    def spread(group, carry):
        here = pl.ds(pl.multiple_of(group * GROUP, GROUP), GROUP)

        def part(first):
            value = rows[here, first * LANES : min((first + 1) * LANES, width)]
            if value.shape[1] < LANES:
                value = jnp.concatenate([value, jnp.zeros((GROUP, LANES - value.shape[1]), jnp.float32)], axis=1)
            return value

        for k in range(COEFFS):
            first, offset = divmod(k * COEFFS, LANES)
            value = part(first)
            if offset + COEFFS > LANES:
                value = jnp.where(lane < offset, part(first + 1), value)
            if offset:
                value = pltpu.roll(value, LANES - offset, 1)
            flat[pl.ds(group * GROUP * LANES + k, GROUP, LANES), :] = jnp.where(lane < COEFFS, value, 0.0)
            if k * BESIDE // COEFFS < (k + 1) * BESIDE // COEFFS:
                gather([groups[group * BESIDE + k * BESIDE // COEFFS]])
        return carry

    lax.fori_loop(0, batches // GROUP, spread, 0)
    each_group(groups, beside, number, gather)
    row = lax.broadcasted_iota(jnp.int32, (size, LANES), 0)

    def product(n, carry):
        here = pl.ds(pl.multiple_of(n * size, size), size)
        value = jnp.where(row < counts[n], held[here, :], 0.0) * signs[...]
        high, low = split(matrix[n].T)
        both[n, :LANES] = high
        both[n, LANES:] = low
        held[here, :] = multiply(value, jnp.concatenate([high, low], axis=0))
        return carry

    lax.fori_loop(0, batches, product, 0, unroll=16)
    save = pltpu.make_async_copy(both, packed, out_sem)
    save.start()
    fetch_sources.wait()
    scatter_rows(groups, number, sources, held, totals)
    totals[0][...] = sum_of(totals) * signs[...]
    every = lane_id((devices, LANES))
    holes = []
    for c in range(CAP):
        value = totals[0][pl.ds(c, devices, CAP), :]
        if c < SPARE:
            holes.append((CAP + c, value))
        else:
            first = 2 * (c - SPARE)
            holes.append((first, jnp.where(every < COEFFS, 0.0, pltpu.roll(value, COEFFS, 1))))
            holes.append((first + 1, jnp.where(every < COEFFS, 0.0, pltpu.roll(value, 2 * COEFFS - LANES, 1))))
    for r in range(ROW_COUNT):
        value = sum([v for place, v in holes if place == r], 0.0)
        there = pl.ds(r, devices, ROW_COUNT)
        message[there, :] = value if r >= CAP else message[there, :] + value
    save.wait()


def near_kernel(
    count, pos, mass, before, after, all_targets, all_sources,
    out,
    extended, lines, choose, ahead, source, target, total, targets, sources, target_sem, source_sem,
):
    fetch_targets = pltpu.make_async_copy(all_targets, targets, target_sem)
    fetch_targets.start()
    fetch_sources = pltpu.make_async_copy(all_sources, sources, source_sem)
    fetch_sources.start()
    rows = mass.shape[0]
    wide = lane_id((rows, LANES))
    for c in range(4):
        own = pos[c] if c < 3 else mass[...]
        extended[c, rows : extended.shape[1], :] = jnp.zeros((extended.shape[1] - rows, LANES), jnp.float32)
        extended[c, 1 : rows + 1, :] = own
        extended[c, 0:1, :] = before[c : c + 1, :]
        extended[c, rows + 1 : rows + 2, :] = after[c : c + 1, :]
        if c < 3:
            swapped = pltpu.roll(own, LEAF, 1)
            ahead[c, pl.ds(0, rows, 2), :] = jnp.where(wide < LEAF, own, swapped)
            ahead[c, pl.ds(1, rows, 2), :] = jnp.where(wide < LEAF, swapped, own)
    k_id = lax.broadcasted_iota(jnp.int32, (2 * LANES, 2 * LANES), 0)
    n_id = lax.broadcasted_iota(jnp.int32, (2 * LANES, 2 * LANES), 1)
    k_in = k_id % LANES
    code = (k_in // (3 * GROUP)) * GROUP + k_in % GROUP - n_id // LANES * GROUP
    code = jnp.where(k_id // LANES == n_id % LANES // LEAF, code, -1)
    tiles = choose.shape[0]

    def make_choice(tile, carry):
        wanted = tile // GROUP * 2 * GROUP + tile % GROUP
        choose[tile] = (code == wanted).astype(jnp.float32).astype(jnp.bfloat16)
        return carry

    lax.fori_loop(0, tiles, make_choice, 0)
    blocks = lines.shape[0] // LEAF
    for block in range(blocks):
        parts = []
        for c in range(4):
            value = extended[c, block * GROUP : (block + 1) * GROUP, :]
            for _ in range(2):
                high = value.astype(jnp.bfloat16).astype(jnp.float32)
                parts.append(high)
                value = value - high
            parts.append(value)
        parts.append(jnp.zeros((LANES - 12 * GROUP, LANES), jnp.float32))
        turned = jnp.concatenate(parts, axis=0).T.astype(jnp.bfloat16)
        quarter = LEAF // 2
        for parity in range(2):
            there = slice(block * LEAF + parity * quarter, block * LEAF + (parity + 1) * quarter)
            lines[there, :LANES] = turned[parity * LEAF : parity * LEAF + quarter]
            lines[there, LANES:] = turned[parity * LEAF + quarter : (parity + 1) * LEAF]
    share = blocks // 3

    def spread(step, carry):
        tile, third = step % tiles, step // tiles
        pair_of, r = tile // GROUP, tile % GROUP
        size = share * LEAF
        some = lines[pl.ds(pl.multiple_of(third * size, size), size), :]
        wide = jnp.dot(some, choose[tile], preferred_element_type=jnp.float32)
        for i in range(share):
            for parity in range(2):
                for q in range(4):
                    first = i * LEAF + parity * 32 + q * GROUP
                    leaf = 2 * ((third * share + i) * GROUP + r) + parity
                    for c in range(2):
                        source[leaf, (2 * pair_of + c) * 4 + q] = wide[first : first + GROUP, c * LANES : (c + 1) * LANES]
        return carry

    lax.fori_loop(0, 3 * tiles, spread, 0, unroll=4)

    def spread_target(leaf, carry):
        for c in range(3):
            target[leaf, c] = jnp.broadcast_to(ahead[c, pl.ds(leaf, 1), :], (GROUP, LANES))
        return carry

    lax.fori_loop(0, 2 * rows, spread_target, 0, unroll=4)
    total[...] = jnp.zeros_like(total)

    def pair(here, there):
        x, y, z = target[here, 0], target[here, 1], target[here, 2]
        parts = []
        for q in range(4):
            dx = x - source[there, q]
            dy = y - source[there, 4 + q]
            dz = z - source[there, 8 + q]
            distance = dx * dx + dy * dy + dz * dz
            inverse = jnp.where(distance > 0.0, lax.rsqrt(distance + SOFTENING), 0.0)
            parts.append(inverse * source[there, 12 + q])
        return here, (parts[0] + parts[1]) + (parts[2] + parts[3])

    later_target, later_source = views(targets, PAIRS), views(sources, PAIRS)

    def several(group, carry):
        first = group * PAIRS
        done = [pair(later_target[i][first], later_source[i][first]) for i in range(PAIRS)]
        for here, value in done:
            total[here] = total[here] + value
        return carry

    fetch_targets.wait()
    fetch_sources.wait()
    live = count[0]
    turns = (live + PAIRS - 1) // PAIRS

    def fill(j, carry):
        sources[j] = source.shape[0] - 1
        return carry

    lax.fori_loop(live, turns * PAIRS, fill, 0)
    lax.fori_loop(0, turns, several, 0)
    summed = sum_sublanes(total.reshape(2 * rows * GROUP, LANES), 2 * rows)
    ahead[0] = summed + pltpu.roll(summed, LEAF, 1)
    out[...] = -jnp.where(wide < LEAF, ahead[0, pl.ds(0, rows, 2), :], ahead[0, pl.ds(1, rows, 2), :])


def back_kernel(
    counts, groups, slots, pos, near, rows_in, packed, all_sources, all_targets,
    out,
    table, returned, both, held, expansion, turned, terms, sources, targets, *rest,
):
    *totals, matrix_sem, source_sem, target_sem = rest
    batches = both.shape[0]
    size = held.shape[0] // batches
    rows = near.shape[0]
    fetch_sources = pltpu.make_async_copy(all_sources, sources, source_sem)
    fetch_sources.start()
    fetch_targets = pltpu.make_async_copy(all_targets, targets, target_sem)
    fetch_targets.start()
    fetch_matrix = pltpu.make_async_copy(packed, both, matrix_sem)
    fetch_matrix.start()
    for c in range(3):
        turned[c] = pos[c].T
    number = groups[groups.shape[0] - 1]
    devices = rows_in.shape[0] // ROW_COUNT
    every = lane_id((devices, LANES))

    def received(r):
        return rows_in[pl.ds(r, devices, ROW_COUNT), :]

    for c in range(CAP):
        table[pl.ds(c, devices, CAP), :] = received(c)
        if c < SPARE:
            value = received(CAP + c)
        else:
            first = 2 * (c - SPARE)
            early = pltpu.roll(received(first), LANES - COEFFS, 1)
            late = pltpu.roll(received(first + 1), 2 * (LANES - COEFFS), 1)
            value = jnp.where(every < LANES - COEFFS, early, late)
        returned[c * devices : (c + 1) * devices, :] = value
    fetch_sources.wait()
    each_group(groups, 0, number, gather_step(sources, table, held))
    fetch_matrix.wait()
    row = lax.broadcasted_iota(jnp.int32, (size, LANES), 0)

    def product(n, carry):
        here = pl.ds(pl.multiple_of(n * size, size), size)
        held[here, :] = multiply(jnp.where(row < counts[n], held[here, :], 0.0), both[n])
        return carry

    lax.fori_loop(0, batches, product, 0, unroll=16)
    fetch_targets.wait()
    scatter_rows(groups, number, targets, held, totals)
    chunk = slots.shape[1]
    leaf = lax.broadcasted_iota(jnp.int32, (expansion.shape[0], chunk), 0)
    sums = sum_of(totals)
    for block in range(slots.shape[0]):
        hot = (leaf == slots[block : block + 1, :]).astype(jnp.float32).astype(jnp.bfloat16)
        high, low = split(returned[block * chunk : (block + 1) * chunk, :])
        sums = sums + jnp.dot(hot, high, preferred_element_type=jnp.float32)
        sums = sums + jnp.dot(hot, low, preferred_element_type=jnp.float32)
    expansion[...] = sums
    for half in range(2):
        terms[half] = expansion[pl.ds(half, rows, 2), :].T
    for half, here in blocks_of(rows):
        sums = [jnp.zeros((LEAF, LANES), jnp.float32)]

        def visit(k, value, half=half, here=here, sums=sums):
            sums[0] = sums[0] + value * terms[half, k : k + 1, here[1]]

        walk(*centred(turned, here), jnp.ones((LEAF, LANES), jnp.float32), visit)
        turned[(3,) + here] = sums[0]
    out[...] = near[...] + turned[3].T


VMEM = pl.BlockSpec(memory_space=pltpu.VMEM)
SMEM = pl.BlockSpec(memory_space=pltpu.SMEM)
ANY = pl.BlockSpec(memory_space=pl.ANY)


def shape(*dims):
    return jax.ShapeDtypeStruct(dims, jnp.float32)


def params(mib):
    return pltpu.CompilerParams(vmem_limit_bytes=mib * MIB)


def scratch(*dims, dtype=jnp.float32):
    return pltpu.VMEM(dims, dtype)


def front(slots, classes, counts, targets, sources, pos, mass, operators, devices):
    rows = mass.shape[0]
    batches, pairs = classes.shape[0], targets.shape[0]
    most = pairs // ROWS + pairs // batches // ROWS + 1
    return pl.pallas_call(
        front_kernel,
        out_shape=(
            shape(devices * ROW_COUNT, LANES),
            jax.ShapeDtypeStruct((-(-most // 1024) * 1024,), jnp.int32),
            jax.ShapeDtypeStruct((batches, 2 * LANES, LANES), jnp.bfloat16),
        ),
        in_specs=[SMEM] * 2 + [VMEM] * 3 + [ANY] * 4,
        out_specs=(VMEM, SMEM, ANY),
        scratch_shapes=[
            scratch(4, LANES, rows),
            scratch(2, LANES, rows),
            scratch(2, rows // LANES, COEFFS * GROUP, LANES),
            scratch(2 * rows, LANES),
            scratch(batches, operators.shape[1]),
            scratch(batches, LANES, LANES),
            scratch(batches, 2 * LANES, LANES, dtype=jnp.bfloat16),
            scratch(pairs, LANES),
            pltpu.SMEM(slots.shape, jnp.int32),
            pltpu.SMEM((pairs,), jnp.int32),
            pltpu.SMEM((pairs,), jnp.int32),
        ]
        + [scratch(slots.size, LANES)] * ACCS
        + [pltpu.SemaphoreType.DMA] * 5,
        compiler_params=params(58),
        name="front",
    )(classes, counts, jnp.asarray(SIGNS), pos, mass, operators, slots, targets, sources)


def back(counts, groups, sources, targets, slots, pos, near, packed, message):
    rows = near.shape[0]
    pairs = sources.shape[0]
    return pl.pallas_call(
        back_kernel,
        out_shape=shape(rows, LANES),
        in_specs=[SMEM] * 2 + [VMEM] * 4 + [ANY] * 3,
        out_specs=VMEM,
        scratch_shapes=[
            scratch(slots.size, LANES),
            scratch(slots.size, LANES),
            scratch(*packed.shape, dtype=jnp.bfloat16),
            scratch(pairs, LANES),
            scratch(2 * rows, LANES),
            scratch(4, LANES, rows),
            scratch(2, LANES, rows),
            pltpu.SMEM((pairs,), jnp.int32),
            pltpu.SMEM((pairs,), jnp.int32),
        ]
        + [scratch(2 * rows, LANES)] * ACCS
        + [pltpu.SemaphoreType.DMA] * 3,
        compiler_params=params(62),
        name="back",
    )(counts, groups, slots, pos, near, message, packed, sources, targets)


def near_field(targets, sources, count, pos, mass, before, after):
    rows = mass.shape[0]
    blocks = -(-(rows + 2) // (3 * GROUP)) * 3
    return pl.pallas_call(
        near_kernel,
        out_shape=shape(rows, LANES),
        in_specs=[SMEM] + [VMEM] * 4 + [ANY] * 2,
        out_specs=VMEM,
        scratch_shapes=[
            scratch(4, blocks * GROUP, LANES),
            scratch(blocks * LEAF, 2 * LANES, dtype=jnp.bfloat16),
            scratch(2 * GROUP, 2 * LANES, 2 * LANES, dtype=jnp.bfloat16),
            scratch(3, 2 * rows, LANES),
            scratch(2 * blocks * GROUP, 16, GROUP, LANES),
            scratch(2 * rows, 3, GROUP, LANES),
            scratch(2 * rows, GROUP, LANES),
            pltpu.SMEM(targets.shape, jnp.int32),
            pltpu.SMEM(sources.shape, jnp.int32),
            pltpu.SemaphoreType.DMA,
            pltpu.SemaphoreType.DMA,
        ],
        compiler_params=params(58),
        name="near_field",
    )(count, pos, mass, before, after, targets, sources)


AXES = ("group", "dom")


def exchange(value):
    devices = lax.axis_size("group") * lax.axis_size("dom")
    blocks = value.reshape(devices, -1, 1, LANES)
    return lax.all_to_all(blocks, AXES, split_axis=0, concat_axis=0, tiled=True).reshape(value.shape)


def shift(value, forward):
    count = lax.axis_size("group") * lax.axis_size("dom")
    pairs = [(i, i + 1) for i in range(count - 1)] if forward else [(i + 1, i) for i in range(count - 1)]
    return lax.ppermute(value, AXES, pairs)


def local(
    positions,
    masses,
    near_target,
    near_source,
    near_count,
    far_target,
    far_source,
    far_class,
    far_count,
    export_slots,
    operators,
):
    devices = lax.axis_size("group") * lax.axis_size("dom")
    slots = export_slots.T
    pos = positions.reshape(3, -1, LANES)
    mass = masses.reshape(-1, LANES)
    ends = jnp.concatenate([pos[:, :: mass.shape[0] - 1], mass[None, :: mass.shape[0] - 1]], axis=0)
    before = shift(ends[:, 1], True)
    after = shift(ends[:, 0], False)
    message, groups, packed = front(slots, far_class, far_count, far_target, far_source, pos, mass, operators, devices)
    message, before, after = lax.optimization_barrier((message, before, after))
    message = exchange(message)
    near = near_field(near_target, near_source, near_count, pos, mass, before, after)
    out = back(far_count, groups, far_source, far_target, slots, pos, near, packed, message)
    return out.reshape(-1)


def solution(mesh):
    split_all = P(AXES)
    in_specs = (P(None, AXES),) + (split_all,) * 8 + (P(AXES, None), P())
    return jax.shard_map(local, mesh=mesh, in_specs=in_specs, out_specs=split_all, check_vma=False)
```

```python
import functools

import jax
import jax.numpy as jnp
import numpy as np
from jax import lax
from jax.experimental import pallas as pl
from jax.experimental.pallas import tpu as pltpu
from jax.sharding import PartitionSpec as P

LEAF = 64
ORDER = 6
LANES = 128
SOFTENING = 0.01
ACCS = 8
GROUP = 8
ROWS = 16
PAIRS = 64
JOINT = 4
BESIDE = 32
CAP = 8
ROW_COUNT = 11
SPARE = ROW_COUNT - CAP
MIB = 1 << 20


def exponent_table(degree_max):
    triples = []
    for degree in range(degree_max + 1):
        for first_pow in range(degree, -1, -1):
            for second_pow in range(degree - first_pow, -1, -1):
                triples.append((first_pow, second_pow, degree - first_pow - second_pow))
    return triples


TRIPLES = exponent_table(ORDER)
COEFFS = len(TRIPLES)
INDEX = {triple: k for k, triple in enumerate(TRIPLES)}
SIGNS = np.ones((1, LANES), np.float32)
SIGNS[0, :COEFFS] = [(-1.0) ** sum(triple) for triple in TRIPLES]


def split(value):
    high = value.astype(jnp.bfloat16)
    return high, (value - high.astype(jnp.float32)).astype(jnp.bfloat16)


def lane_id(shape):
    return lax.broadcasted_iota(jnp.int32, shape, len(shape) - 1)


def walk(x, y, z, start, visit):
    along_x = start
    for a in range(ORDER + 1):
        along_y = along_x
        for b in range(ORDER + 1 - a):
            along_z = along_y
            for c in range(ORDER + 1 - a - b):
                visit(INDEX[(a, b, c)], along_z)
                if c < ORDER - a - b:
                    along_z = along_z * z
            if b < ORDER - a:
                along_y = along_y * y
        if a < ORDER:
            along_x = along_x * x


def sum_sublanes(value, count):
    return functools.reduce(lambda a, b: a + b, [value[pl.ds(i, count, GROUP), :] for i in range(GROUP)])


def centred(turned, here):
    u = []
    for c in range(3):
        value = turned[(c,) + here]
        u.append(value - jnp.sum(value, axis=0, keepdims=True) * (1.0 / LEAF))
    return u


def block_of(here):
    return here[1].start // LANES


def blocks_of(rows):
    for half in range(2):
        for block in range(rows // LANES):
            yield half, (slice(half * LEAF, (half + 1) * LEAF), slice(block * LANES, (block + 1) * LANES))


def list_groups(counts, batches, size, groups):
    share = size // ROWS
    later = [groups.at[pl.ds(i, groups.shape[0] - share + 1)] for i in range(share)]

    def one(n, place):
        for i in range(share):
            later[i][place] = n * size + i * ROWS
        return place + (counts[n] + ROWS - 1) // ROWS

    return lax.fori_loop(0, batches, one, 0, unroll=4)


def each_group(groups, start, number, step):
    def several(turn, carry):
        step([groups[turn * JOINT + i] for i in range(JOINT)])
        return carry

    def single(turn, carry):
        step([groups[turn]])
        return carry

    lax.fori_loop(start // JOINT, number // JOINT, several, 0)
    lax.fori_loop(jnp.maximum(number // JOINT * JOINT, start), number, single, 0)


def views(index, width):
    return [index.at[pl.ds(i, index.shape[0] - width + 1)] for i in range(width)]


def gather_step(index, table, held):
    later = views(index, ROWS)

    def step(firsts):
        for first in firsts:
            rows = [table[pl.ds(later[i][first], 1), :] for i in range(ROWS)]
            for i in range(ROWS):
                held[pl.ds(first + i, 1), :] = rows[i]

    return step


def scatter_rows(groups, number, index, held, totals):
    for total in totals:
        total[...] = jnp.zeros_like(total)

    later = views(index, ROWS)

    def step(firsts):
        for first in firsts:
            for i in range(ROWS):
                total = totals[i % len(totals)]
                there = pl.ds(later[i][first], 1)
                total[there, :] = total[there, :] + held[pl.ds(first + i, 1), :]

    each_group(groups, 0, number, step)


def sum_of(totals):
    return functools.reduce(lambda a, b: a + b, [total[...] for total in totals])


def dot(a, b):
    return jnp.dot(a, b, preferred_element_type=jnp.float32)


def multiply(value, both):
    high, low = split(value)
    upper, lower = both[:LANES], both[LANES:]
    square = jnp.concatenate(
        [jnp.concatenate([upper, lower], axis=1), jnp.concatenate([upper, jnp.zeros_like(lower)], axis=1)], axis=0
    )
    wide = dot(jnp.concatenate([high, low], axis=1), square)
    return wide[:, :LANES] + wide[:, LANES:]


def front_kernel(
    classes, counts, signs, pos, mass, operators, all_slots, all_targets, all_sources,
    message, groups, packed,
    turned, terms, parts, table, rows, matrix, both, held, slots, targets, sources, *rest,
):
    *totals, row_sem, out_sem, slot_sem, target_sem, source_sem = rest
    batches = rows.shape[0]
    size = held.shape[0] // batches
    leaf_rows = mass.shape[0]

    fetch_slots = pltpu.make_async_copy(all_slots, slots, slot_sem)
    fetch_slots.start()
    fetch_targets = pltpu.make_async_copy(all_targets, targets, target_sem)
    fetch_targets.start()
    fetch_sources = pltpu.make_async_copy(all_sources, sources, source_sem)
    fetch_sources.start()

    def fetch(n):
        return pltpu.make_async_copy(operators.at[pl.ds(classes[n], 1), :], rows.at[pl.ds(n, 1), :], row_sem)

    lax.fori_loop(0, batches, lambda n, c: (fetch(n).start(), c)[1], 0, unroll=8)
    for c in range(3):
        turned[c] = pos[c].T
    turned[3] = mass[...].T
    terms[...] = jnp.zeros_like(terms)
    for half, here in blocks_of(leaf_rows):

        def visit(k, value, half=half, here=here):
            whole = functools.reduce(lambda a, b: a + b, [value[i : i + GROUP] for i in range(0, LEAF, GROUP)])
            parts[half, block_of(here), k * GROUP : (k + 1) * GROUP, :] = whole

        walk(*centred(turned, here), turned[(3,) + here], visit)
    for half in range(2):
        for block in range(leaf_rows // LANES):
            terms[half, :COEFFS, block * LANES : (block + 1) * LANES] = sum_sublanes(parts.at[half, block], COEFFS)
        table[pl.ds(half, leaf_rows, 2), :] = terms[half].T
    devices = message.shape[0] // ROW_COUNT
    fetch_slots.wait()

    def export(device, carry):
        values = [table[pl.ds(slots[c, device], 1), :] for c in range(CAP)]
        for c in range(CAP):
            message[pl.ds(device * ROW_COUNT + c, 1), :] = values[c]
        return carry

    lax.fori_loop(0, devices, export, 0, unroll=8)
    number = list_groups(counts, batches, size, groups)
    groups[groups.shape[0] - 1] = number
    fetch_targets.wait()
    gather = gather_step(targets, table, held)
    beside = BESIDE * batches // GROUP

    def fill(place, carry):
        groups[place] = 0
        return carry

    lax.fori_loop(number, beside, fill, 0)
    lax.fori_loop(0, batches, lambda n, c: (fetch(n).wait(), c)[1], 0, unroll=8)
    lane = lane_id((GROUP, LANES))
    width = rows.shape[1]
    flat = matrix.reshape(batches * LANES, LANES)
    matrix[:, COEFFS:, :] = jnp.zeros((batches, LANES - COEFFS, LANES), jnp.float32)

    def spread(group, carry):
        here = pl.ds(pl.multiple_of(group * GROUP, GROUP), GROUP)

        def part(first):
            value = rows[here, first * LANES : min((first + 1) * LANES, width)]
            if value.shape[1] < LANES:
                value = jnp.concatenate([value, jnp.zeros((GROUP, LANES - value.shape[1]), jnp.float32)], axis=1)
            return value

        for k in range(COEFFS):
            first, offset = divmod(k * COEFFS, LANES)
            value = part(first)
            if offset + COEFFS > LANES:
                value = jnp.where(lane < offset, part(first + 1), value)
            if offset:
                value = pltpu.roll(value, LANES - offset, 1)
            flat[pl.ds(group * GROUP * LANES + k, GROUP, LANES), :] = jnp.where(lane < COEFFS, value, 0.0)
            if k * BESIDE // COEFFS < (k + 1) * BESIDE // COEFFS:
                gather([groups[group * BESIDE + k * BESIDE // COEFFS]])
        return carry

    lax.fori_loop(0, batches // GROUP, spread, 0)
    each_group(groups, beside, number, gather)
    row = lax.broadcasted_iota(jnp.int32, (size, LANES), 0)

    def product(n, carry):
        here = pl.ds(pl.multiple_of(n * size, size), size)
        value = jnp.where(row < counts[n], held[here, :], 0.0) * signs[...]
        high, low = split(matrix[n].T)
        both[n, :LANES] = high
        both[n, LANES:] = low
        held[here, :] = multiply(value, jnp.concatenate([high, low], axis=0))
        return carry

    lax.fori_loop(0, batches, product, 0, unroll=16)
    save = pltpu.make_async_copy(both, packed, out_sem)
    save.start()
    fetch_sources.wait()
    scatter_rows(groups, number, sources, held, totals)
    totals[0][...] = sum_of(totals) * signs[...]
    every = lane_id((devices, LANES))
    holes = []
    for c in range(CAP):
        value = totals[0][pl.ds(c, devices, CAP), :]
        if c < SPARE:
            holes.append((CAP + c, value))
        else:
            first = 2 * (c - SPARE)
            holes.append((first, jnp.where(every < COEFFS, 0.0, pltpu.roll(value, COEFFS, 1))))
            holes.append((first + 1, jnp.where(every < COEFFS, 0.0, pltpu.roll(value, 2 * COEFFS - LANES, 1))))
    for r in range(ROW_COUNT):
        value = sum([v for place, v in holes if place == r], 0.0)
        there = pl.ds(r, devices, ROW_COUNT)
        message[there, :] = value if r >= CAP else message[there, :] + value
    save.wait()


def near_kernel(
    count, pos, mass, before, after, all_targets, all_sources,
    out,
    extended, lines, choose, ahead, source, target, total, targets, sources, target_sem, source_sem,
):
    fetch_targets = pltpu.make_async_copy(all_targets, targets, target_sem)
    fetch_targets.start()
    fetch_sources = pltpu.make_async_copy(all_sources, sources, source_sem)
    fetch_sources.start()
    rows = mass.shape[0]
    wide = lane_id((rows, LANES))
    for c in range(4):
        own = pos[c] if c < 3 else mass[...]
        extended[c, rows : extended.shape[1], :] = jnp.zeros((extended.shape[1] - rows, LANES), jnp.float32)
        extended[c, 1 : rows + 1, :] = own
        extended[c, 0:1, :] = before[c : c + 1, :]
        extended[c, rows + 1 : rows + 2, :] = after[c : c + 1, :]
        if c < 3:
            swapped = pltpu.roll(own, LEAF, 1)
            ahead[c, pl.ds(0, rows, 2), :] = jnp.where(wide < LEAF, own, swapped)
            ahead[c, pl.ds(1, rows, 2), :] = jnp.where(wide < LEAF, swapped, own)
    k_id = lax.broadcasted_iota(jnp.int32, (2 * LANES, 2 * LANES), 0)
    n_id = lax.broadcasted_iota(jnp.int32, (2 * LANES, 2 * LANES), 1)
    k_in = k_id % LANES
    code = (k_in // (3 * GROUP)) * GROUP + k_in % GROUP - n_id // LANES * GROUP
    code = jnp.where(k_id // LANES == n_id % LANES // LEAF, code, -1)
    tiles = choose.shape[0]

    def make_choice(tile, carry):
        wanted = tile // GROUP * 2 * GROUP + tile % GROUP
        choose[tile] = (code == wanted).astype(jnp.float32).astype(jnp.bfloat16)
        return carry

    lax.fori_loop(0, tiles, make_choice, 0)
    blocks = lines.shape[0] // LEAF
    for block in range(blocks):
        parts = []
        for c in range(4):
            value = extended[c, block * GROUP : (block + 1) * GROUP, :]
            for _ in range(2):
                high = value.astype(jnp.bfloat16).astype(jnp.float32)
                parts.append(high)
                value = value - high
            parts.append(value)
        parts.append(jnp.zeros((LANES - 12 * GROUP, LANES), jnp.float32))
        turned = jnp.concatenate(parts, axis=0).T.astype(jnp.bfloat16)
        quarter = LEAF // 2
        for parity in range(2):
            there = slice(block * LEAF + parity * quarter, block * LEAF + (parity + 1) * quarter)
            lines[there, :LANES] = turned[parity * LEAF : parity * LEAF + quarter]
            lines[there, LANES:] = turned[parity * LEAF + quarter : (parity + 1) * LEAF]
    share = blocks // 3

    def spread(step, carry):
        tile, third = step % tiles, step // tiles
        pair_of, r = tile // GROUP, tile % GROUP
        size = share * LEAF
        some = lines[pl.ds(pl.multiple_of(third * size, size), size), :]
        wide = jnp.dot(some, choose[tile], preferred_element_type=jnp.float32)
        for i in range(share):
            for parity in range(2):
                for q in range(4):
                    first = i * LEAF + parity * 32 + q * GROUP
                    leaf = 2 * ((third * share + i) * GROUP + r) + parity
                    for c in range(2):
                        source[leaf, (2 * pair_of + c) * 4 + q] = wide[first : first + GROUP, c * LANES : (c + 1) * LANES]
        return carry

    lax.fori_loop(0, 3 * tiles, spread, 0, unroll=4)

    def spread_target(leaf, carry):
        for c in range(3):
            target[leaf, c] = jnp.broadcast_to(ahead[c, pl.ds(leaf, 1), :], (GROUP, LANES))
        return carry

    lax.fori_loop(0, 2 * rows, spread_target, 0, unroll=4)
    total[...] = jnp.zeros_like(total)

    def pair(here, there):
        x, y, z = target[here, 0], target[here, 1], target[here, 2]
        parts = []
        for q in range(4):
            dx = x - source[there, q]
            dy = y - source[there, 4 + q]
            dz = z - source[there, 8 + q]
            distance = dx * dx + dy * dy + dz * dz
            inverse = jnp.where(distance > 0.0, lax.rsqrt(distance + SOFTENING), 0.0)
            parts.append(inverse * source[there, 12 + q])
        return here, (parts[0] + parts[1]) + (parts[2] + parts[3])

    later_target, later_source = views(targets, PAIRS), views(sources, PAIRS)

    def several(group, carry):
        first = group * PAIRS
        done = [pair(later_target[i][first], later_source[i][first]) for i in range(PAIRS)]
        for here, value in done:
            total[here] = total[here] + value
        return carry

    fetch_targets.wait()
    fetch_sources.wait()
    live = count[0]
    turns = (live + PAIRS - 1) // PAIRS

    def fill(j, carry):
        sources[j] = source.shape[0] - 1
        return carry

    lax.fori_loop(live, turns * PAIRS, fill, 0)
    lax.fori_loop(0, turns, several, 0)
    summed = sum_sublanes(total.reshape(2 * rows * GROUP, LANES), 2 * rows)
    ahead[0] = summed + pltpu.roll(summed, LEAF, 1)
    out[...] = -jnp.where(wide < LEAF, ahead[0, pl.ds(0, rows, 2), :], ahead[0, pl.ds(1, rows, 2), :])


def back_kernel(
    counts, groups, slots, pos, near, rows_in, packed, all_sources, all_targets,
    out,
    table, returned, both, held, expansion, turned, terms, sources, targets, *rest,
):
    *totals, matrix_sem, source_sem, target_sem = rest
    batches = both.shape[0]
    size = held.shape[0] // batches
    rows = near.shape[0]
    fetch_sources = pltpu.make_async_copy(all_sources, sources, source_sem)
    fetch_sources.start()
    fetch_targets = pltpu.make_async_copy(all_targets, targets, target_sem)
    fetch_targets.start()
    fetch_matrix = pltpu.make_async_copy(packed, both, matrix_sem)
    fetch_matrix.start()
    for c in range(3):
        turned[c] = pos[c].T
    number = groups[groups.shape[0] - 1]
    devices = rows_in.shape[0] // ROW_COUNT
    every = lane_id((devices, LANES))

    def received(r):
        return rows_in[pl.ds(r, devices, ROW_COUNT), :]

    for c in range(CAP):
        table[pl.ds(c, devices, CAP), :] = received(c)
        if c < SPARE:
            value = received(CAP + c)
        else:
            first = 2 * (c - SPARE)
            early = pltpu.roll(received(first), LANES - COEFFS, 1)
            late = pltpu.roll(received(first + 1), 2 * (LANES - COEFFS), 1)
            value = jnp.where(every < LANES - COEFFS, early, late)
        returned[c * devices : (c + 1) * devices, :] = value
    fetch_sources.wait()
    each_group(groups, 0, number, gather_step(sources, table, held))
    fetch_matrix.wait()
    row = lax.broadcasted_iota(jnp.int32, (size, LANES), 0)

    def product(n, carry):
        here = pl.ds(pl.multiple_of(n * size, size), size)
        held[here, :] = multiply(jnp.where(row < counts[n], held[here, :], 0.0), both[n])
        return carry

    lax.fori_loop(0, batches, product, 0, unroll=16)
    fetch_targets.wait()
    scatter_rows(groups, number, targets, held, totals)
    chunk = slots.shape[1]
    leaf = lax.broadcasted_iota(jnp.int32, (expansion.shape[0], chunk), 0)
    sums = sum_of(totals)
    for block in range(slots.shape[0]):
        hot = (leaf == slots[block : block + 1, :]).astype(jnp.float32).astype(jnp.bfloat16)
        high, low = split(returned[block * chunk : (block + 1) * chunk, :])
        sums = sums + jnp.dot(hot, high, preferred_element_type=jnp.float32)
        sums = sums + jnp.dot(hot, low, preferred_element_type=jnp.float32)
    expansion[...] = sums
    for half in range(2):
        terms[half] = expansion[pl.ds(half, rows, 2), :].T
    for half, here in blocks_of(rows):
        sums = [jnp.zeros((LEAF, LANES), jnp.float32)]

        def visit(k, value, half=half, here=here, sums=sums):
            sums[0] = sums[0] + value * terms[half, k : k + 1, here[1]]

        walk(*centred(turned, here), jnp.ones((LEAF, LANES), jnp.float32), visit)
        turned[(3,) + here] = sums[0]
    out[...] = near[...] + turned[3].T


VMEM = pl.BlockSpec(memory_space=pltpu.VMEM)
SMEM = pl.BlockSpec(memory_space=pltpu.SMEM)
ANY = pl.BlockSpec(memory_space=pl.ANY)


def shape(*dims):
    return jax.ShapeDtypeStruct(dims, jnp.float32)


def params(mib):
    return pltpu.CompilerParams(vmem_limit_bytes=mib * MIB)


def scratch(*dims, dtype=jnp.float32):
    return pltpu.VMEM(dims, dtype)


def front(slots, classes, counts, targets, sources, pos, mass, operators, devices):
    rows = mass.shape[0]
    batches, pairs = classes.shape[0], targets.shape[0]
    most = pairs // ROWS + pairs // batches // ROWS + 1
    return pl.pallas_call(
        front_kernel,
        out_shape=(
            shape(devices * ROW_COUNT, LANES),
            jax.ShapeDtypeStruct((-(-most // 1024) * 1024,), jnp.int32),
            jax.ShapeDtypeStruct((batches, 2 * LANES, LANES), jnp.bfloat16),
        ),
        in_specs=[SMEM] * 2 + [VMEM] * 3 + [ANY] * 4,
        out_specs=(VMEM, SMEM, ANY),
        scratch_shapes=[
            scratch(4, LANES, rows),
            scratch(2, LANES, rows),
            scratch(2, rows // LANES, COEFFS * GROUP, LANES),
            scratch(2 * rows, LANES),
            scratch(batches, operators.shape[1]),
            scratch(batches, LANES, LANES),
            scratch(batches, 2 * LANES, LANES, dtype=jnp.bfloat16),
            scratch(pairs, LANES),
            pltpu.SMEM(slots.shape, jnp.int32),
            pltpu.SMEM((pairs,), jnp.int32),
            pltpu.SMEM((pairs,), jnp.int32),
        ]
        + [scratch(slots.size, LANES)] * ACCS
        + [pltpu.SemaphoreType.DMA] * 5,
        compiler_params=params(58),
        name="front",
    )(classes, counts, jnp.asarray(SIGNS), pos, mass, operators, slots, targets, sources)


def back(counts, groups, sources, targets, slots, pos, near, packed, message):
    rows = near.shape[0]
    pairs = sources.shape[0]
    return pl.pallas_call(
        back_kernel,
        out_shape=shape(rows, LANES),
        in_specs=[SMEM] * 2 + [VMEM] * 4 + [ANY] * 3,
        out_specs=VMEM,
        scratch_shapes=[
            scratch(slots.size, LANES),
            scratch(slots.size, LANES),
            scratch(*packed.shape, dtype=jnp.bfloat16),
            scratch(pairs, LANES),
            scratch(2 * rows, LANES),
            scratch(4, LANES, rows),
            scratch(2, LANES, rows),
            pltpu.SMEM((pairs,), jnp.int32),
            pltpu.SMEM((pairs,), jnp.int32),
        ]
        + [scratch(2 * rows, LANES)] * ACCS
        + [pltpu.SemaphoreType.DMA] * 3,
        compiler_params=params(63),
        name="back",
    )(counts, groups, slots, pos, near, message, packed, sources, targets)


def near_field(targets, sources, count, pos, mass, before, after):
    rows = mass.shape[0]
    blocks = -(-(rows + 2) // (3 * GROUP)) * 3
    return pl.pallas_call(
        near_kernel,
        out_shape=shape(rows, LANES),
        in_specs=[SMEM] + [VMEM] * 4 + [ANY] * 2,
        out_specs=VMEM,
        scratch_shapes=[
            scratch(4, blocks * GROUP, LANES),
            scratch(blocks * LEAF, 2 * LANES, dtype=jnp.bfloat16),
            scratch(2 * GROUP, 2 * LANES, 2 * LANES, dtype=jnp.bfloat16),
            scratch(3, 2 * rows, LANES),
            scratch(2 * blocks * GROUP, 16, GROUP, LANES),
            scratch(2 * rows, 3, GROUP, LANES),
            scratch(2 * rows, GROUP, LANES),
            pltpu.SMEM(targets.shape, jnp.int32),
            pltpu.SMEM(sources.shape, jnp.int32),
            pltpu.SemaphoreType.DMA,
            pltpu.SemaphoreType.DMA,
        ],
        compiler_params=params(58),
        name="near_field",
    )(count, pos, mass, before, after, targets, sources)


AXES = ("group", "dom")


def exchange(value):
    devices = lax.axis_size("group") * lax.axis_size("dom")
    blocks = value.reshape(devices, -1, 1, LANES)
    return lax.all_to_all(blocks, AXES, split_axis=0, concat_axis=0, tiled=True).reshape(value.shape)


def shift(value, forward):
    count = lax.axis_size("group") * lax.axis_size("dom")
    pairs = [(i, i + 1) for i in range(count - 1)] if forward else [(i + 1, i) for i in range(count - 1)]
    return lax.ppermute(value, AXES, pairs)


def local(
    positions,
    masses,
    near_target,
    near_source,
    near_count,
    far_target,
    far_source,
    far_class,
    far_count,
    export_slots,
    operators,
):
    devices = lax.axis_size("group") * lax.axis_size("dom")
    slots = export_slots.T
    pos = positions.reshape(3, -1, LANES)
    mass = masses.reshape(-1, LANES)
    ends = jnp.concatenate([pos[:, :: mass.shape[0] - 1], mass[None, :: mass.shape[0] - 1]], axis=0)
    before = shift(ends[:, 1], True)
    after = shift(ends[:, 0], False)
    message, groups, packed = front(slots, far_class, far_count, far_target, far_source, pos, mass, operators, devices)
    message, before, after = lax.optimization_barrier((message, before, after))
    message = exchange(message)
    near = near_field(near_target, near_source, near_count, pos, mass, before, after)
    out = back(far_count, groups, far_source, far_target, slots, pos, near, packed, message)
    return out.reshape(-1)


def solution(mesh):
    split_all = P(AXES)
    in_specs = (P(None, AXES),) + (split_all,) * 8 + (P(AXES, None), P())
    return jax.shard_map(local, mesh=mesh, in_specs=in_specs, out_specs=split_all, check_vma=False)
```
